512 devices in a mesh: tm: 8 (over x, z_hi), space: 64 (over z_lo, y, core).
Axes of the slice: x: 4, y: 4, z: 16 (z_hi: 2, z_lo: 8; z = z_hi * 8 + z_lo), core: 2. Of those that a mesh axis runs over, the one named last changes fastest.
Arguments:
- initial: float32 [5, 64, 8192], P(None, None, 'space'), may hold values from -6 to 6
- neighbours: int32 [6, 8192], P(None, 'space'), may hold values from 0 to 8191, as said below
- volume_op: float32 [64, 64], replicated, may hold values from -0.75 to 0.75
- lift_op: float32 [64, 96], replicated, may hold values from -0.625 to 0.625
- coarse_volume: float32 [8, 8], replicated, may hold values from -2 to 2
- coarse_lift: float32 [8, 24], replicated, may hold values from -2.25 to 2.25
- mixing: float32 [5, 5], replicated, may hold values from -2.5 to 2.5
- restrict_op: float32 [8, 64], replicated, may hold values from -0.75 to 0.75
- prolong_op: float32 [64, 8], replicated, may hold values from -2 to 2
Outputs:
- slice_ends: float32 [8, 5, 64, 8192], P('tm', None, None, 'space')
The draws below stay inside these ranges and needn't reach their ends.
Inputs may be any that keep to these rules, and one draw needn't show every extreme that they name: Elements are numbered layer by layer, 64 to a layer; a layer is a periodic 8 x 8 grid in shuffled order; entries 0..3 name the neighbours along x and y in the same layer, entries 4 and 5 the element at the same grid place in the layer below and above, periodic over all layers.
All inputs are finite; a program needn't handle non-finite values.
Results may differ from the reference program's by a relative error of at most 0.0001.
Values sent between devices are 32-bit elements; how exact they have to be, the bound alone decides.
No kernel may reach another device: no remote copies, remote signals or barrier semaphores. Data moves between devices by JAX's collectives and lax.ppermute only.
A program may use at most 64 MiB of HBM per device.

```python
import jax
import jax.numpy as jnp
from jax import lax

FIELDS = 5
NODES = 64
COARSE_NODES = 8
ITERS = 2
LAYER_SIDE = 8
LAYER = 64
ELEMS = 8192
N_TM = 8


def draw_neighbours(key, part):
    key = jax.random.fold_in(key, 7)
    layers = ELEMS // LAYER
    keys = jax.random.split(key, layers)
    orders = jax.vmap(lambda sub: jax.random.permutation(sub, LAYER))(keys).astype(jnp.int32)
    inverse = jnp.argsort(orders, axis=1).astype(jnp.int32)
    position = inverse.reshape(-1)
    layer_of = jnp.arange(ELEMS, dtype=jnp.int32) // LAYER
    row_of = position // LAYER_SIDE
    col_of = position % LAYER_SIDE

    def element_at(layer_no, row_no, col_no):
        layer_no = layer_no % layers
        place = row_no % LAYER_SIDE * LAYER_SIDE + col_no % LAYER_SIDE
        return layer_no * LAYER + orders[layer_no, place]
    result = jnp.stack([element_at(layer_of, row_of - 1, col_of), element_at(layer_of, row_of + 1, col_of), element_at(layer_of, row_of, col_of - 1), element_at(layer_of, row_of, col_of + 1), element_at(layer_of - 1, row_of, col_of), element_at(layer_of + 1, row_of, col_of)])
    return result.astype(jnp.int32)


def draw_coarse_lift(key, part):
    key = jax.random.fold_in(key, 11)
    side_key, face_key = jax.random.split(key, 2)
    side = jnp.clip(jax.random.normal(side_key, (COARSE_NODES, 16), jnp.float32) * 24.0 ** (-0.5), -1.2, 1.2)
    face = jnp.clip(jax.random.normal(face_key, (COARSE_NODES, 8), jnp.float32) * 0.75, -2.25, 2.25)
    return jnp.concatenate([side, face], axis=1).astype(jnp.float32)


def block_scale(own_key, extent, cuts, least, high):
    factor_of, own = 1.0, jax.random.fold_in(own_key, 6)
    for dim, parts in cuts:
        heights = jnp.exp(jax.random.uniform(jax.random.fold_in(own, dim), (parts,), jnp.float32, least / len(cuts), high / len(cuts)))
        factor_of = factor_of * jnp.repeat(heights, extent[dim] // parts).reshape([-1 if axis == dim else 1 for axis in range(len(extent))])
    return factor_of


def centred(stream_key, shape, spread, most, cuts=(), kind=jnp.bfloat16):
    loudness = block_scale(stream_key, shape, cuts, -0.22, 0.18) if cuts else 1.0
    values = jax.random.normal(stream_key, shape, jnp.float32) * spread * loudness
    return jnp.minimum(jnp.maximum(values, -most), most).astype(kind)


def setup_inputs(seed: int = 0) -> dict:
    key_of = jax.random.split(jax.random.key(seed), 10)
    initial = centred(key_of[0], (FIELDS, NODES, ELEMS), 1.0, 6.0, ((2, 64),), jnp.float32)
    neighbours = draw_neighbours(jax.random.fold_in(key_of[9], 71), 0)
    volume_op = centred(key_of[2], (NODES, NODES), NODES ** -0.5, 0.75, (), jnp.float32)
    lift_op = centred(key_of[3], (NODES, 96), 96 ** -0.5, 0.625, (), jnp.float32)
    coarse_volume = centred(key_of[4], (COARSE_NODES, COARSE_NODES), COARSE_NODES ** -0.5, 2.0, (), jnp.float32)
    coarse_lift = draw_coarse_lift(jax.random.fold_in(key_of[9], 71), 0)
    mixing = centred(key_of[6], (FIELDS, FIELDS), FIELDS ** -0.5, 2.5, (), jnp.float32)
    restrict_op = centred(key_of[7], (COARSE_NODES, NODES), NODES ** -0.5, 0.75, (), jnp.float32)
    prolong_op = centred(key_of[8], (NODES, COARSE_NODES), COARSE_NODES ** -0.5, 2.0, (), jnp.float32)
    return dict(initial=initial, neighbours=neighbours, volume_op=volume_op, lift_op=lift_op, coarse_volume=coarse_volume, coarse_lift=coarse_lift, mixing=mixing, restrict_op=restrict_op, prolong_op=prolong_op)


exact_mode = lax.Precision.HIGHEST
time_step = 0.125


def traces(state, per_edge):
    leading = state.shape[:-2]
    elements = state.shape[-1]
    cubed = state.reshape(leading + (per_edge, per_edge, per_edge, elements))
    surfaces = [cubed[..., per_edge - 1, :, :, :], cubed[..., 0, :, :, :],
                cubed[..., :, per_edge - 1, :, :], cubed[..., :, 0, :, :],
                cubed[..., :, :, per_edge - 1, :], cubed[..., :, :, 0, :]]
    return [surface.reshape(leading + (per_edge * per_edge, elements)) for surface in surfaces]


def apply_nodes(matrix, state):
    return jnp.einsum('ij,...je->...ie', matrix, state, precision=exact_mode)


def rate(state, neighbours, volume_op, lift_op, mixing, per_edge):
    surfaces = traces(state, per_edge)
    pieces = [jnp.take(surfaces[which], neighbours[which], axis=-1) for which in range(6)]
    stacked = jnp.concatenate(pieces, axis=-2)
    inner = apply_nodes(volume_op, state) + apply_nodes(lift_op, stacked)
    return jnp.einsum('cd,...die->...cie', mixing, inner, precision=exact_mode)


def coarse_sweep(begin, begin_rate, prev_head, prev_tail, defect):
    return begin + time_step * (begin_rate - prev_head) + time_step * (prev_head + prev_tail) / 2 + defect


def reference(initial, neighbours, volume_op, lift_op, coarse_volume, coarse_lift, mixing, restrict_op, prolong_op):
    def fine(state):
        return rate(state, neighbours, volume_op, lift_op, mixing, 4)

    def coarse(state):
        return rate(state, neighbours, coarse_volume, coarse_lift, mixing, 2)

    start_rate = fine(initial)
    shape_all = (N_TM,) + initial.shape
    head_state = jnp.broadcast_to(initial, shape_all)
    mid_state = head_state
    end_state = head_state
    head_rate = jnp.broadcast_to(start_rate, shape_all)
    mid_rate = head_rate
    end_rate = head_rate
    for step in range(ITERS):
        if step > 0:
            head_state = jnp.concatenate([initial[None], end_state[:-1]], axis=0)
            head_rate = jnp.concatenate([start_rate[None], end_rate[:-1]], axis=0)
        old_head = apply_nodes(restrict_op, head_state)
        old_tail = apply_nodes(restrict_op, end_state)
        old_head_rate = coarse(old_head)
        old_tail_rate = coarse(old_tail)
        integral = time_step * (head_rate + 4.0 * mid_rate + end_rate) / 6.0
        defect = apply_nodes(restrict_op, integral) - time_step * (old_head_rate + old_tail_rate) / 2
        carry = old_head[0]
        begins, tails, heads, tail_rates = [], [], [], []
        for position in range(N_TM):
            begin = carry
            head = coarse(begin)
            prev_head, prev_tail = old_head_rate[position], old_tail_rate[position]
            for sweep in range(2):
                tail = coarse_sweep(begin, head, prev_head, prev_tail, defect[position])
                tail_rate = coarse(tail)
                prev_head, prev_tail = head, tail_rate
            begins.append(begin)
            tails.append(tail)
            heads.append(head)
            tail_rates.append(tail_rate)
            carry = tail
        new_head = jnp.stack(begins)
        new_tail = jnp.stack(tails)
        new_head_rate = jnp.stack(heads)
        new_tail_rate = jnp.stack(tail_rates)
        delta_head = new_head - old_head
        delta_tail = new_tail - old_tail
        head_state = head_state + apply_nodes(prolong_op, delta_head)
        mid_state = mid_state + apply_nodes(prolong_op, (delta_head + delta_tail) / 2)
        end_state = end_state + apply_nodes(prolong_op, delta_tail)
        rate_head = new_head_rate - old_head_rate
        rate_tail = new_tail_rate - old_tail_rate
        head_rate = head_rate + apply_nodes(prolong_op, rate_head)
        mid_rate = mid_rate + apply_nodes(prolong_op, (rate_head + rate_tail) / 2)
        end_rate = end_rate + apply_nodes(prolong_op, rate_tail)
        fresh_head = fine(head_state)
        fresh_mid = head_state + time_step / 2 * (fresh_head - head_rate) + time_step * (5.0 * head_rate + 8.0 * mid_rate - end_rate) / 24.0
        fresh_mid_rate = fine(fresh_mid)
        fresh_end = fresh_mid + time_step / 2 * (fresh_mid_rate - mid_rate) + time_step * (-head_rate + 8.0 * mid_rate + 5.0 * end_rate) / 24.0
        if step + 1 < ITERS:
            end_rate_next = fine(fresh_end)
        else:
            end_rate_next = end_rate
        head_rate, mid_rate, end_rate = fresh_head, fresh_mid_rate, end_rate_next
        mid_state, end_state = fresh_mid, fresh_end
    return end_state
```

```python
import functools

import jax
import jax.numpy as jnp
from jax import lax
from jax.experimental import pallas as pl
from jax.experimental.pallas import tpu as pltpu
from jax.sharding import PartitionSpec as P

LAYER = 64
FIELDS = 5
DT = 0.125
HALF = 0.7071067811865476
EXACT = lax.Precision.HIGHEST
F32 = jnp.float32
VMEM_LIMIT = 48 * 1024 * 1024


def iota(shape, dim):
    return lax.broadcasted_iota(jnp.int32, shape, dim)


def nn(a, b):
    return lax.dot_general(a, b, (((1,), (0,)), ((), ())), precision=EXACT, preferred_element_type=F32)


def nt(a, b):
    return lax.dot_general(a, b, (((1,), (1,)), ((), ())), precision=EXACT, preferred_element_type=F32)


def eighth_cos(turn):
    turn = turn & 7
    diagonal = jnp.where((turn == 1) | (turn == 7), HALF, jnp.where((turn == 3) | (turn == 5), -HALF, 0.0))
    return jnp.where(turn == 0, 1.0, jnp.where(turn == 4, -1.0, diagonal)).astype(F32)


def wave_numbers(unit):
    low = unit - 23
    high = unit - 26
    kx = jnp.where(unit < 24, unit & 7, jnp.where(unit < 27, low, jnp.where(unit < 30, high, 0)))
    ky = jnp.where(unit < 24, 1 + (unit >> 3), jnp.where(unit < 27, 0, jnp.where(unit == 30, 0, 4)))
    paired = jnp.where(unit < 30, 1, 0)
    kx_other = jnp.where(unit < 30, kx, 4)
    return kx, ky, kx_other, ky, paired


def to_modes_kernel(initial_ref, neighbours_ref, sent_ref, basis_ref):
    place = lax.axis_index("space")
    total = lax.axis_size("space") * 2 * LAYER
    base = place * 2 * LAYER
    lane = iota((1, 128), 1)
    upper = lane >= LAYER
    beside = neighbours_ref[...]
    target = iota((128, 128), 0)

    def steps(face):
        one = jnp.where(beside[face : face + 1] - base == target, 1.0, 0.0).astype(jnp.bfloat16)
        two = jnp.dot(one, one, preferred_element_type=F32).astype(jnp.bfloat16)
        four = jnp.dot(two, two, preferred_element_type=F32).astype(jnp.bfloat16)
        return one, two, four

    row = iota((8, 128), 0)
    found = jnp.where((row == 0) & ((iota((8, 128), 1) & (LAYER - 1)) == 0), 1.0, 0.0).astype(F32)
    for part, moves in ((1, steps(0)), (2, steps(2))):
        for power, move in enumerate(moves):
            shifted = jnp.dot(found.astype(jnp.bfloat16), move, preferred_element_type=F32)
            found = found + shifted + jnp.where(row == part, shifted[0:1] * (1 << power), 0.0)
    along_x = found[1:2]
    along_y = found[2:3]

    below = jnp.where(upper, base, (base + total - LAYER) % total)
    hit = beside[4:5] == below
    extra = jnp.zeros((1, 128), F32)
    for slot, (layer_upper, value) in enumerate(
        ((False, along_x), (False, along_y), (True, along_x), (True, along_y))
    ):
        part = jnp.where(hit & (upper == layer_upper), value, 0.0)
        extra = jnp.where(lane == slot, jnp.sum(part, axis=1, keepdims=True), extra)

    mode = iota((LAYER, 128), 0)
    kx, ky, kx_other, ky_other, paired = wave_numbers(mode >> 1)
    second = (mode & 1) == 1
    turns = (
        jnp.where(second, kx_other, kx) * along_x.astype(jnp.int32)
        + jnp.where(second, ky_other, ky) * along_y.astype(jnp.int32)
        + jnp.where(second, 2 * paired, 0)
    )
    basis = eighth_cos(turns)
    basis_ref[...] = basis
    for field in range(FIELDS):
        state = initial_ref[field]
        apart = jnp.concatenate([jnp.where(upper, 0.0, state), jnp.where(upper, state, 0.0)], axis=0)
        sent_ref[:, field * 128 : (field + 1) * 128] = nt(basis, apart)
    sent_ref[:, FIELDS * 128 :] = jnp.broadcast_to(extra, (LAYER, 128))


def from_modes_kernel(modes_ref, basis_ref, out_ref):
    mode = iota((LAYER, 128), 0)
    scale = jnp.where(mode < 60, 2.0 / LAYER, 1.0 / LAYER).astype(F32)
    back = basis_ref[...] * scale
    upper = iota((LAYER, 128), 1) >= LAYER
    for field in range(FIELDS):
        part = jnp.transpose(modes_ref[:, field * 128 : (field + 1) * 128])
        whole = nn(part, back)
        out_ref[0, field] = jnp.where(upper, whole[LAYER:], whole[:LAYER])


def beside_layers(state, from_below):
    even, odd = state[:LAYER], state[LAYER:]
    return jnp.concatenate(
        [
            jnp.where(from_below, pltpu.roll(odd, 1, 0), odd),
            jnp.where(from_below, even, pltpu.roll(even, LAYER - 1, 0)),
        ],
        axis=0,
    )


def face_weights(shape, per_edge, node, weights):
    column = iota(shape, 1)
    face = column // (per_edge * per_edge)
    trace = column % (per_edge * per_edge)
    a, b, c = (node // (per_edge * per_edge), (node // per_edge) % per_edge, node % per_edge)
    first = [a, a, b, b, c, c]
    rest = [b * per_edge + c] * 2 + [a * per_edge + c] * 2 + [a * per_edge + b] * 2
    result = jnp.zeros(shape, F32)
    for which, weight in weights.items():
        edge = per_edge - 1 if which % 2 == 0 else 0
        on = (face == which) & (first[which] == edge) & (rest[which] == trace)
        result = jnp.where(on, weight, result)
    return result


def iterate_kernel(
    slices,
    received_ref,
    volume_ref,
    lift_ref,
    coarse_volume_ref,
    coarse_lift_ref,
    mixing_ref,
    mixing_smem,
    restrict_ref,
    prolong_ref,
    sent_ref,
    fine_op,
    coarse_op,
    restrict_all,
    prolong_all,
    start,
    start_rate,
    before,
    before_rate,
    mid_rate,
    end_rate,
    chain,
    chain_rate,
    ends,
    ends_rate,
    mids,
    ends_coarse_rate,
):
    place = lax.axis_index("space")
    mine = lax.axis_index("tm")
    core = place & 1
    kx, ky, kx_other, ky_other, paired = wave_numbers(place >> 1)
    single = paired == 0

    def turn_cos(first, second, second_half):
        return jnp.where(second_half, eighth_cos(second), eighth_cos(first))

    wide = iota((128, 128), 1)
    tall = iota((128, 128), 0)
    row = iota((128, 96), 0)
    half = row >= 64
    same = (wide >= 64) == (tall >= 64)
    cos_x = turn_cos(kx, kx_other, half)
    cos_y = turn_cos(ky, ky_other, half)
    sin_x = jnp.where(single, 0.0, eighth_cos(kx - 2))
    sin_y = jnp.where(single, 0.0, eighth_cos(ky - 2))
    sign = jnp.where(half, -1.0, 1.0)
    along = face_weights((128, 96), 4, row & 63, {0: cos_x, 1: cos_x, 2: cos_y, 3: cos_y})
    across = face_weights(
        (128, 96), 4, row & 63, {0: -sin_x * sign, 1: sin_x * sign, 2: -sin_y * sign, 3: sin_y * sign}
    )
    ahead = face_weights((128, 96), 4, row & 63, {4: 1.0, 5: 1.0})
    lift2 = jnp.concatenate([lift_ref[...]] * 2, axis=0)
    volume2 = jnp.concatenate([volume_ref[...]] * 2, axis=0)
    twice = jnp.where((iota((128, 64), 0) & 63) == iota((128, 64), 1), 1.0, 0.0).astype(F32)
    fine_op[:128] = jnp.where(same, nt(twice, volume2) + nt(along, lift2), nt(across, lift2))
    fine_op[128:] = jnp.where(same, nt(ahead, lift2), 0.0)

    row = iota((128, 24), 0)
    half = ((row >> 3) & 1) == 1
    cos_x = turn_cos(kx, kx_other, half)
    cos_y = turn_cos(ky, ky_other, half)
    sign = jnp.where(half, -1.0, 1.0)
    along = face_weights((128, 24), 2, row & 7, {0: cos_x, 1: cos_x, 2: cos_y, 3: cos_y})
    across = face_weights(
        (128, 24), 2, row & 7, {0: -sin_x * sign, 1: sin_x * sign, 2: -sin_y * sign, 3: sin_y * sign}
    )
    ahead = face_weights((128, 24), 2, row & 7, {4: 1.0, 5: 1.0})
    node8 = jnp.where((iota((128, 8), 0) & 7) == iota((128, 8), 1), 1.0, 0.0).astype(F32)
    field8 = jnp.where((iota((128, FIELDS), 0) >> 4) == iota((128, FIELDS), 1), 1.0, 0.0).astype(F32)
    same = ((wide >> 3) & 1) == ((tall >> 3) & 1)
    clift = coarse_lift_ref[...]
    coupled = nt(nt(field8, mixing_ref[...]), field8)
    along = nt(nt(node8, coarse_volume_ref[...]) + nt(along, clift), node8)
    across = nt(nt(across, clift), node8)
    ahead = nt(nt(ahead, clift), node8)
    coarse_op[:128] = coupled * jnp.where(same, along, across)
    coarse_op[128:] = coupled * jnp.where(same, ahead, 0.0)

    restricting = nt(twice, nn(node8, restrict_ref[...]))
    prolonging = nt(node8, jnp.concatenate([prolong_ref[...]] * 2, axis=0))
    down = (tall >= 64) == (((wide >> 3) & 1) == 1)
    up = (wide >= 64) == (((tall >> 3) & 1) == 1)
    for field in range(FIELDS):
        restrict_all[field * 128 : (field + 1) * 128] = jnp.where(
            down & ((wide >> 4) == field), restricting, 0.0
        )
        prolong_all[:, field * 128 : (field + 1) * 128] = jnp.where(
            up & ((tall >> 4) == field), prolonging, 0.0
        )

    lane = iota((LAYER, 128), 1)
    fine_below = (lane & 3) == 3
    coarse_below = (lane & 1) == 1
    halved = lane >= 64

    def fields_of(state):
        return [state[field * 128 : (field + 1) * 128] for field in range(FIELDS)]

    def fine(state):
        parts = fields_of(state)
        pieces = []
        for field in range(FIELDS):
            mixed = mixing_smem[field, 0] * parts[0]
            for other in range(1, FIELDS):
                mixed = mixed + mixing_smem[field, other] * parts[other]
            pieces.append(jnp.concatenate([mixed, beside_layers(mixed, fine_below)], axis=1))
        return nn(jnp.concatenate(pieces, axis=0), fine_op[...])

    def coarse(state):
        return nn(jnp.concatenate([state, beside_layers(state, coarse_below)], axis=1), coarse_op[...])

    def restrict(state):
        return nn(jnp.concatenate(fields_of(state), axis=1), restrict_all[...])

    def prolong(state):
        wide_state = nn(state, prolong_all[...])
        return jnp.concatenate(
            [wide_state[:, field * 128 : (field + 1) * 128] for field in range(FIELDS)], axis=0
        )

    shifts = received_ref[:LAYER, FIELDS * 128 :]
    lower_triangle = jnp.where(iota((LAYER, LAYER), 1) < iota((LAYER, LAYER), 0), 1.0, 0.0).astype(F32)
    first_x, first_y = shifts[:, 0:1], shifts[:, 1:2]
    both_x, both_y = first_x + shifts[:, 2:3], first_y + shifts[:, 3:4]
    passed_x = nn(lower_triangle, jnp.broadcast_to(both_x, (LAYER, 128)))
    passed_y = nn(lower_triangle, jnp.broadcast_to(both_y, (LAYER, 128)))
    turning = []
    for add_x, add_y in ((first_x, first_y), (both_x, both_y)):
        shift_x = (passed_x + add_x).astype(jnp.int32)
        shift_y = (passed_y + add_y).astype(jnp.int32)
        turns = jnp.where(halved, kx_other, kx) * shift_x + jnp.where(halved, ky_other, ky) * shift_y
        cos = eighth_cos(turns)
        sin = jnp.where(single, 0.0, eighth_cos(turns - 2))
        turning.append((cos, jnp.where(halved, sin, -sin)))

    for field in range(FIELDS):
        real = received_ref[:LAYER, field * 128 : (field + 1) * 128]
        imaginary = received_ref[LAYER:, field * 128 : (field + 1) * 128]
        even = jnp.where(halved, pltpu.roll(imaginary, 64, 1), real)
        odd = jnp.where(halved, imaginary, pltpu.roll(real, 64, 1))
        for index, value in enumerate((even, odd)):
            cos, sin = turning[index]
            begin = field * 128 + index * LAYER
            start[begin : begin + LAYER] = value * cos + pltpu.roll(value, 64, 1) * sin

    def relay(step, first_part, second_part):
        head, head_rate = chain[step], chain_rate[step]
        tail = head + DT * head_rate + first_part
        tail = head + (DT / 2) * (head_rate + coarse(tail)) + second_part
        chain[step + 1] = tail
        chain_rate[step + 1] = coarse(tail)

    initial = start[...]
    start_rate[...] = fine(initial)
    rate = start_rate[...]
    begin = restrict(initial)
    begin_rate = coarse(begin)
    rate_coarse = restrict(rate)
    tau = DT * rate_coarse - DT * begin_rate
    chain[0] = begin
    chain_rate[0] = begin_rate

    def first_relay(step, carry):
        relay(step, tau, tau)
        return carry

    lax.fori_loop(0, slices, first_relay, 0)

    before[...] = initial
    before_rate[...] = rate
    ends[0] = begin
    ends_rate[0] = rate_coarse
    ends_coarse_rate[0] = begin_rate

    def first_sweep(step, carry):
        head, head_rate, tail_rate = chain[step], chain_rate[step], chain_rate[step + 1]
        state = start[...] + prolong(head - begin)
        push = prolong((DT / 8) * (tail_rate - head_rate))
        state = state + (DT / 2) * fine(state) + push
        middle_rate = fine(state)
        state = state + (DT / 2) * middle_rate + push
        last_rate = fine(state)
        coarse_end = restrict(state)
        ends[step + 1] = coarse_end
        mids[step] = restrict(middle_rate)
        ends_rate[step + 1] = restrict(last_rate)
        ends_coarse_rate[step + 1] = coarse(coarse_end)

        @pl.when(step + 1 == mine)
        def _():
            before[...] = state
            before_rate[...] = last_rate

        @pl.when(step == mine)
        def _():
            mid_rate[...] = middle_rate
            end_rate[...] = last_rate

        return carry

    lax.fori_loop(0, slices, first_sweep, 0)

    def second_relay(step, carry):
        integral = (DT / 6) * (ends_rate[step] + 4.0 * mids[step] + ends_rate[step + 1])
        old_head_rate, old_tail_rate = ends_coarse_rate[step], ends_coarse_rate[step + 1]
        relay(step, integral - DT * old_head_rate, integral - (DT / 2) * (old_head_rate + old_tail_rate))
        return carry

    lax.fori_loop(0, slices, second_relay, 0)

    state = before[...] + prolong(chain[mine] - ends[mine])
    push = prolong(
        (DT / 8)
        * (
            (chain_rate[mine + 1] - ends_coarse_rate[mine + 1])
            - (chain_rate[mine] - ends_coarse_rate[mine])
        )
    )
    head_rate, middle_rate, last_rate = before_rate[...], mid_rate[...], end_rate[...]
    state = (
        state
        + (DT / 2) * fine(state)
        + (DT / 24) * (8.0 * middle_rate - 7.0 * head_rate - last_rate)
        + push
    )
    state = (
        state
        + (DT / 2) * fine(state)
        + (DT / 24) * (5.0 * last_rate - 4.0 * middle_rate - head_rate)
        + push
    )
    for field in range(FIELDS):
        halves = []
        for index in range(2):
            cos, sin = turning[index]
            begin_row = field * 128 + index * LAYER
            value = state[begin_row : begin_row + LAYER]
            halves.append(value * cos - pltpu.roll(value, 64, 1) * sin)
        even, odd = halves
        real = jnp.where(halved, pltpu.roll(odd, 64, 1), even)
        imaginary = jnp.where(halved, odd, pltpu.roll(even, 64, 1))
        sent_ref[:, field * 128 : (field + 1) * 128] = jnp.where(core == 0, real, imaginary)


def on_device(
    initial,
    neighbours,
    volume_op,
    lift_op,
    coarse_volume,
    coarse_lift,
    mixing,
    restrict_op,
    prolong_op,
):
    in_vmem = pl.BlockSpec(memory_space=pltpu.VMEM)
    params = pltpu.CompilerParams(vmem_limit_bytes=VMEM_LIMIT)
    sent, basis = pl.pallas_call(
        to_modes_kernel,
        out_shape=(
            jax.ShapeDtypeStruct((LAYER, (FIELDS + 1) * 128), F32),
            jax.ShapeDtypeStruct((LAYER, 128), F32),
        ),
        in_specs=[in_vmem] * 2,
        out_specs=(in_vmem, in_vmem),
        compiler_params=params,
        name="to_modes",
    )(initial, neighbours)
    arrived = lax.all_to_all(sent[:, None, :], "space", 0, 0, tiled=True)
    pairs = [[i, i + 1] for i in range(0, lax.axis_size("space"), 2)]
    pair = lax.all_gather(arrived, "space", axis_index_groups=pairs)
    received = pair.reshape(2 * LAYER, (FIELDS + 1) * 128)

    slices = lax.axis_size("tm")
    fine_shape = pltpu.VMEM((FIELDS * 128, 128), F32)
    coarse_shape = pltpu.VMEM((slices + 1, 128, 128), F32)
    modes = pl.pallas_call(
        functools.partial(iterate_kernel, slices),
        out_shape=jax.ShapeDtypeStruct((LAYER, FIELDS * 128), F32),
        in_specs=[in_vmem] * 6 + [pl.BlockSpec(memory_space=pltpu.SMEM)] + [in_vmem] * 2,
        out_specs=in_vmem,
        scratch_shapes=[
            pltpu.VMEM((256, 128), F32),
            pltpu.VMEM((256, 128), F32),
            pltpu.VMEM((FIELDS * 128, 128), F32),
            pltpu.VMEM((128, FIELDS * 128), F32),
        ]
        + [fine_shape] * 6
        + [coarse_shape] * 6,
        compiler_params=params,
        name="iterate",
    )(
        received,
        volume_op,
        lift_op,
        coarse_volume,
        coarse_lift,
        mixing,
        mixing,
        restrict_op,
        prolong_op,
    )
    returned = lax.all_to_all(modes[:, None, :], "space", 0, 0, tiled=True)
    return pl.pallas_call(
        from_modes_kernel,
        out_shape=jax.ShapeDtypeStruct((1, FIELDS, LAYER, 128), F32),
        in_specs=[in_vmem] * 2,
        out_specs=in_vmem,
        compiler_params=params,
        name="from_modes",
    )(returned.reshape(LAYER, FIELDS * 128), basis)


def solution(mesh):
    return jax.shard_map(
        on_device,
        mesh=mesh,
        in_specs=(P(None, None, "space"), P(None, "space"), P(), P(), P(), P(), P(), P(), P()),
        out_specs=P("tm", None, None, "space"),
        check_vma=False,
    )
```

```python
import functools

import jax
import jax.numpy as jnp
import numpy as np
from jax import lax
from jax.experimental import pallas as pl
from jax.experimental.pallas import tpu as pltpu
from jax.sharding import PartitionSpec as P

LAYER = 64
FIELDS = 5
DT = 0.125
HALF = 0.7071067811865476
EXACT = lax.Precision.HIGHEST
F32 = jnp.float32
BF16 = jnp.bfloat16
VMEM_LIMIT = 48 * 1024 * 1024


def iota(shape, dim):
    return lax.broadcasted_iota(jnp.int32, shape, dim)


def nn(a, b):
    return lax.dot_general(a, b, (((1,), (0,)), ((), ())), precision=EXACT, preferred_element_type=F32)


def nt(a, b):
    return lax.dot_general(a, b, (((1,), (1,)), ((), ())), precision=EXACT, preferred_element_type=F32)


def eighth_cos(turn):
    turn = turn & 7
    diagonal = jnp.where((turn == 1) | (turn == 7), HALF, jnp.where((turn == 3) | (turn == 5), -HALF, 0.0))
    return jnp.where(turn == 0, 1.0, jnp.where(turn == 4, -1.0, diagonal)).astype(F32)


def wave_numbers(unit):
    low = unit - 23
    high = unit - 26
    kx = jnp.where(unit < 24, unit & 7, jnp.where(unit < 27, low, jnp.where(unit < 30, high, 0)))
    ky = jnp.where(unit < 24, 1 + (unit >> 3), jnp.where(unit < 27, 0, jnp.where(unit == 30, 0, 4)))
    paired = jnp.where(unit < 30, 1, 0)
    kx_other = jnp.where(unit < 30, kx, 4)
    return kx, ky, kx_other, ky, paired


def to_modes_kernel(initial_ref, neighbours_ref, sent_ref, basis_ref):
    place = lax.axis_index("space")
    total = lax.axis_size("space") * 2 * LAYER
    base = place * 2 * LAYER
    lane = iota((1, 128), 1)
    upper = lane >= LAYER
    beside = neighbours_ref[...]
    target = iota((128, 128), 0)

    def steps(face):
        one = jnp.where(beside[face : face + 1] - base == target, 1.0, 0.0).astype(jnp.bfloat16)
        two = jnp.dot(one, one, preferred_element_type=F32).astype(jnp.bfloat16)
        four = jnp.dot(two, two, preferred_element_type=F32).astype(jnp.bfloat16)
        return one, two, four

    row = iota((8, 128), 0)
    found = jnp.where((row == 0) & ((iota((8, 128), 1) & (LAYER - 1)) == 0), 1.0, 0.0).astype(F32)
    for part, moves in ((1, steps(0)), (2, steps(2))):
        for power, move in enumerate(moves):
            shifted = jnp.dot(found.astype(jnp.bfloat16), move, preferred_element_type=F32)
            found = found + shifted + jnp.where(row == part, shifted[0:1] * (1 << power), 0.0)
    along_x = found[1:2]
    along_y = found[2:3]

    below = jnp.where(upper, base, (base + total - LAYER) % total)
    hit = beside[4:5] == below
    extra = jnp.zeros((1, 128), F32)
    for slot, (layer_upper, value) in enumerate(
        ((False, along_x), (False, along_y), (True, along_x), (True, along_y))
    ):
        part = jnp.where(hit & (upper == layer_upper), value, 0.0)
        extra = jnp.where(lane == slot, jnp.sum(part, axis=1, keepdims=True), extra)

    mode = iota((LAYER, 128), 0)
    kx, ky, kx_other, ky_other, paired = wave_numbers(mode >> 1)
    second = (mode & 1) == 1
    turns = (
        jnp.where(second, kx_other, kx) * along_x.astype(jnp.int32)
        + jnp.where(second, ky_other, ky) * along_y.astype(jnp.int32)
        + jnp.where(second, 2 * paired, 0)
    )
    basis = eighth_cos(turns)
    basis_ref[...] = basis
    for field in range(FIELDS):
        state = initial_ref[field]
        apart = jnp.concatenate([jnp.where(upper, 0.0, state), jnp.where(upper, state, 0.0)], axis=0)
        sent_ref[:, field * 128 : (field + 1) * 128] = nt(basis, apart)
    sent_ref[:, FIELDS * 128 :] = jnp.broadcast_to(extra, (LAYER, 128))


def from_modes_kernel(modes_ref, basis_ref, out_ref):
    mode = iota((LAYER, 128), 0)
    scale = jnp.where(mode < 60, 2.0 / LAYER, 1.0 / LAYER).astype(F32)
    back = basis_ref[...] * scale
    upper = iota((LAYER, 128), 1) >= LAYER
    for field in range(FIELDS):
        part = jnp.transpose(modes_ref[:, field * 128 : (field + 1) * 128])
        whole = nn(part, back)
        out_ref[0, field] = jnp.where(upper, whole[LAYER:], whole[:LAYER])


SHIFTS_A = (0, 1, -1, 2, -2)
SHIFTS_B = (0, 1, -1)
FAR_A = (3, -3)
FAR_B = (2, -2)
NEAR = len(SHIFTS_A) + len(SHIFTS_B)
BLOCKS = NEAR + len(FAR_A) + len(FAR_B)
RING = 8


def face_weights(shape, per_edge, node, weights):
    column = iota(shape, 1)
    face = column // (per_edge * per_edge)
    trace = column % (per_edge * per_edge)
    a, b, c = (node // (per_edge * per_edge), (node // per_edge) % per_edge, node % per_edge)
    first = [a, a, b, b, c, c]
    rest = [b * per_edge + c] * 2 + [a * per_edge + c] * 2 + [a * per_edge + b] * 2
    result = jnp.zeros(shape, F32)
    for which, weight in weights.items():
        edge = per_edge - 1 if which % 2 == 0 else 0
        on = (face == which) & (first[which] == edge) & (rest[which] == trace)
        result = jnp.where(on, weight, result)
    return result


def split(value):
    high = value.astype(BF16)
    return high, (value - high.astype(F32)).astype(BF16)


def bdot(a, b):
    return jnp.dot(a, b, preferred_element_type=F32)


def operators_kernel(
    volume_ref,
    lift_ref,
    coarse_volume_ref,
    coarse_lift_ref,
    mixing_ref,
    restrict_ref,
    prolong_ref,
    fine_ref,
    chain_high_ref,
    chain_low_ref,
    restrict_all_ref,
    prolong_high_ref,
    prolong_low_ref,
    near_high_ref,
    near_low_ref,
    far_ref,
):
    place = lax.axis_index("space")
    kx, ky, kx_other, ky_other, paired = wave_numbers(place >> 1)
    single = paired == 0

    def turn_cos(first, second, second_half):
        return jnp.where(second_half, eighth_cos(second), eighth_cos(first))

    def put_packed(ref, rows, value):
        high, low = split(value)
        ref[rows, :128] = high
        ref[rows, 128:] = low

    def put(high_ref, low_ref, rows, columns, value):
        high, low = split(value)
        high_ref[rows, columns] = high
        low_ref[rows, columns] = low

    wide = iota((128, 128), 1)
    tall = iota((128, 128), 0)
    row = iota((128, 96), 0)
    half = row >= 64
    same = (wide >= 64) == (tall >= 64)
    cos_x = turn_cos(kx, kx_other, half)
    cos_y = turn_cos(ky, ky_other, half)
    sin_x = jnp.where(single, 0.0, eighth_cos(kx - 2))
    sin_y = jnp.where(single, 0.0, eighth_cos(ky - 2))
    sign = jnp.where(half, -1.0, 1.0)
    along = face_weights((128, 96), 4, row & 63, {0: cos_x, 1: cos_x, 2: cos_y, 3: cos_y})
    across = face_weights(
        (128, 96), 4, row & 63, {0: -sin_x * sign, 1: sin_x * sign, 2: -sin_y * sign, 3: sin_y * sign}
    )
    ahead = face_weights((128, 96), 4, row & 63, {4: 1.0, 5: 1.0})
    lift2 = jnp.concatenate([lift_ref[...]] * 2, axis=0)
    volume2 = jnp.concatenate([volume_ref[...]] * 2, axis=0)
    twice = jnp.where((iota((128, 64), 0) & 63) == iota((128, 64), 1), 1.0, 0.0).astype(F32)
    inside = (DT / 2) * jnp.where(same, nt(twice, volume2) + nt(along, lift2), nt(across, lift2))
    beside = (DT / 2) * jnp.where(same, nt(ahead, lift2), 0.0)
    put_packed(fine_ref, slice(0, 128), inside)
    put_packed(fine_ref, slice(128, 256), beside)
    psi = jnp.concatenate([inside, beside], axis=0)

    row = iota((128, 24), 0)
    half = ((row >> 3) & 1) == 1
    cos_x = turn_cos(kx, kx_other, half)
    cos_y = turn_cos(ky, ky_other, half)
    sign = jnp.where(half, -1.0, 1.0)
    along = face_weights((128, 24), 2, row & 7, {0: cos_x, 1: cos_x, 2: cos_y, 3: cos_y})
    across = face_weights(
        (128, 24), 2, row & 7, {0: -sin_x * sign, 1: sin_x * sign, 2: -sin_y * sign, 3: sin_y * sign}
    )
    ahead = face_weights((128, 24), 2, row & 7, {4: 1.0, 5: 1.0})
    node8 = jnp.where((iota((128, 8), 0) & 7) == iota((128, 8), 1), 1.0, 0.0).astype(F32)
    field8 = jnp.where((iota((128, FIELDS), 0) >> 4) == iota((128, FIELDS), 1), 1.0, 0.0).astype(F32)
    same = ((wide >> 3) & 1) == ((tall >> 3) & 1)
    clift = coarse_lift_ref[...]
    mixing = mixing_ref[...]
    power = nt(field8, mixing)
    coupled = [nt(field8, field8), nt(power, field8)]
    for _ in range(2):
        power = nt(power, mixing)
        coupled.append(nt(power, field8))
    along = nt(nt(node8, coarse_volume_ref[...]) + nt(along, clift), node8)
    across = nt(nt(across, clift), node8)
    ahead = nt(nt(ahead, clift), node8)
    level = DT * coupled[1] * jnp.where(same, along, across)
    beside = DT * coupled[1] * jnp.where(same, ahead, 0.0)
    upper = (tall & 1) == 1
    below = jnp.where(upper, beside, 0.0)
    above = jnp.where(upper, 0.0, beside)
    level_level = nn(level, level)
    below_all = nn(below, jnp.concatenate([level, below, above], axis=1))
    above_all = nn(above, jnp.concatenate([level, below, above], axis=1))
    once = [level, below, above, jnp.zeros((128, 128), F32)]
    squared = [
        level_level + below_all[:, 256:] + above_all[:, 128:256],
        nn(level, below) + below_all[:, :128],
        nn(level, above) + above_all[:, :128],
        below_all[:, 128:256] + above_all[:, 256:],
    ]
    for block in range(4):
        rows = slice(block * 128, (block + 1) * 128)
        put(chain_high_ref, chain_low_ref, rows, slice(0, 128), once[block])
        put(chain_high_ref, chain_low_ref, rows, slice(128, 256), 0.5 * squared[block])

    restricting = nt(twice, nn(node8, restrict_ref[...]))
    prolonging = nt(node8, jnp.concatenate([prolong_ref[...]] * 2, axis=0))
    down = (tall >= 64) == (((wide >> 3) & 1) == 1)
    up = (wide >= 64) == (((tall >> 3) & 1) == 1)
    restricting = jnp.where(down, restricting, 0.0)
    prolonging = jnp.where(up, prolonging, 0.0)
    for field in range(FIELDS):
        part = slice(field * 128, (field + 1) * 128)
        put_packed(restrict_all_ref, part, jnp.where((wide >> 4) == field, restricting, 0.0))
        put(prolong_high_ref, prolong_low_ref, slice(0, 128), part, jnp.where((tall >> 4) == field, prolonging, 0.0))

    response = jnp.where(tall < 16, prolonging, 0.0)
    fine_below = (wide & 3) == 3
    responses = [nn(response, restricting)]
    for _ in range(3):
        near = jnp.where(fine_below, pltpu.roll(response, 16, 0), pltpu.roll(response, 112, 0))
        response = nn(jnp.concatenate([response, near], axis=1), psi)
        responses.append(nn(response, restricting))

    def block(shift, weights):
        rows = slice((shift % RING) * 16, (shift % RING) * 16 + 16)
        total = jnp.zeros((128, 128), F32)
        for order, weight in weights.items():
            if abs(shift) <= order:
                total = total + weight * coupled[order] * jnp.concatenate([responses[order][rows]] * 8, axis=0)
        return total

    kinds = [(shift, 0) for shift in SHIFTS_A] + [(shift, 1) for shift in SHIFTS_B]
    kinds += [(shift, 0) for shift in FAR_A] + [(shift, 1) for shift in FAR_B]
    ends = ({0: 1.0, 1: 2.0, 2: 1.0}, {0: 2.0, 1: 1.0})
    mid_rates = ({1: 1.0, 2: 1.0}, {1: 1.0})
    end_rates = ({1: 1.0, 2: 2.0, 3: 1.0}, {1: 2.0, 2: 1.0})
    for index, (shift, kind) in enumerate(kinds):
        rows = slice(index * 128, (index + 1) * 128)
        if index < NEAR:
            put(near_high_ref, near_low_ref, rows, slice(0, 128), block(shift, ends[kind]))
            put(near_high_ref, near_low_ref, rows, slice(128, 256), block(shift, mid_rates[kind]))
        put_packed(far_ref, rows, block(shift, end_rates[kind]))


def shifted(even, odd, shift):
    def rolled(value, by):
        return value if by == 0 else pltpu.roll(value, by % LAYER, 0)

    if shift % 2 == 0:
        return rolled(even, shift // 2), rolled(odd, shift // 2)
    return rolled(odd, (shift + 1) // 2), rolled(even, (shift - 1) // 2)


def beside_layers(state, from_below, reach=1):
    even, odd = state[:LAYER], state[LAYER:]
    below = shifted(even, odd, reach)
    above = shifted(even, odd, -reach)
    return jnp.concatenate([jnp.where(from_below, low, high) for low, high in zip(below, above)], axis=0)


def moved(state, shift):
    return jnp.concatenate(shifted(state[:LAYER], state[LAYER:], shift), axis=0)


def polynomials():
    once = np.array([1.0, 1.0])
    twice = np.polymul(once, once)
    two = np.array([1.0, 2.0])
    on_start = np.array([5 / 12, 4 / 3, 1.0])
    on_mid = np.array([2 / 3, 1 / 3, 0.0])
    on_end = np.array([-1 / 12, 1 / 3, 0.0])
    own = np.polyadd(np.polymul(on_mid, once), np.polymul(on_end, twice))
    table = {
        "first": np.polyadd(on_start, own),
        "later": np.polyadd(np.polymul(on_start, twice), own),
        "head": own,
        "push": np.polyadd(on_mid, np.polymul(on_end, two)),
        "head_before": np.polymul(on_start, twice),
        "push_before": np.polymul(on_start, two),
        "new_head": twice,
        "new_push": two,
    }
    return {name: [float(x) for x in np.pad(p[::-1], (0, 5 - len(p)))] for name, p in table.items()}


def iterate_kernel(
    slices,
    received_ref,
    fine_ref,
    chain_high_ref,
    chain_low_ref,
    restrict_all_ref,
    prolong_high_ref,
    prolong_low_ref,
    near_high_ref,
    near_low_ref,
    far_ref,
    mixing_smem,
    sent_ref,
    start,
    head1,
    rate1,
    head2,
    rate2,
    ends,
    ends_rate,
    left_high,
    left_low,
):
    place = lax.axis_index("space")
    mine = lax.axis_index("tm")
    core = place & 1
    kx, ky, kx_other, ky_other, paired = wave_numbers(place >> 1)
    single = paired == 0
    lane = iota((LAYER, 128), 1)
    fine_below = (lane & 3) == 3
    coarse_below = (lane & 1) == 1
    halved = lane >= 64

    def packed_dot(value, packed):
        high, low = split(value)
        both = bdot(high, packed)
        return both[:, :128] + (both[:, 128:] + bdot(low, packed[:, :128]))

    def dot3(value, high_op, low_op):
        high, low = split(value)
        return bdot(high, high_op) + (bdot(high, low_op) + bdot(low, high_op))

    def fields_of(state):
        return [state[field * 128 : (field + 1) * 128] for field in range(FIELDS)]

    def psi(state):
        parts = fields_of(state)
        pieces = []
        for field in range(FIELDS):
            mixed = mixing_smem[field, 0] * parts[0]
            for other in range(1, FIELDS):
                mixed = mixed + mixing_smem[field, other] * parts[other]
            pieces.append(jnp.concatenate([mixed, beside_layers(mixed, fine_below)], axis=1))
        return packed_dot(jnp.concatenate(pieces, axis=0), fine_ref[...])

    def restrict(state):
        return packed_dot(jnp.concatenate(fields_of(state), axis=1), restrict_all_ref[...])

    def stage(state):
        wide = [state, moved(state, 1), moved(state, -1), beside_layers(state, coarse_below, 2)]
        both = dot3(jnp.concatenate(wide, axis=1), chain_high_ref[...], chain_low_ref[...])
        return both[:, :128], both[:, 128:]

    shifts = received_ref[:LAYER, FIELDS * 128 :]
    lower_triangle = jnp.where(iota((LAYER, LAYER), 1) < iota((LAYER, LAYER), 0), 1.0, 0.0).astype(F32)
    first_x, first_y = shifts[:, 0:1], shifts[:, 1:2]
    both_x, both_y = first_x + shifts[:, 2:3], first_y + shifts[:, 3:4]
    passed_x = nn(lower_triangle, jnp.broadcast_to(both_x, (LAYER, 128)))
    passed_y = nn(lower_triangle, jnp.broadcast_to(both_y, (LAYER, 128)))
    turning = []
    for add_x, add_y in ((first_x, first_y), (both_x, both_y)):
        shift_x = (passed_x + add_x).astype(jnp.int32)
        shift_y = (passed_y + add_y).astype(jnp.int32)
        turns = jnp.where(halved, kx_other, kx) * shift_x + jnp.where(halved, ky_other, ky) * shift_y
        cos = eighth_cos(turns)
        sin = jnp.where(single, 0.0, eighth_cos(turns - 2))
        turning.append((cos, jnp.where(halved, sin, -sin)))

    for field in range(FIELDS):
        real = received_ref[:LAYER, field * 128 : (field + 1) * 128]
        imaginary = received_ref[LAYER:, field * 128 : (field + 1) * 128]
        even = jnp.where(halved, pltpu.roll(imaginary, 64, 1), real)
        odd = jnp.where(halved, imaginary, pltpu.roll(real, 64, 1))
        for index, value in enumerate((even, odd)):
            cos, sin = turning[index]
            begin = field * 128 + index * LAYER
            start[begin : begin + LAYER] = value * cos + pltpu.roll(value, 64, 1) * sin

    initial = start[...]
    power = psi(initial)
    begin = restrict(initial)
    power_coarse = [begin, restrict(power)]
    for _ in range(2):
        power = psi(power)
        power_coarse.append(restrict(power))
    begin_rate, begin_twice = stage(begin)
    defect = 2.0 * power_coarse[1] - begin_rate
    head, rate = begin, begin_rate
    head1[0] = head
    rate1[0] = rate
    for step in range(slices):
        once, half_twice = stage(rate + defect)
        head, rate = head + rate + defect + 0.5 * once, rate + once + half_twice
        head1[step + 1] = head
        rate1[step + 1] = rate
        change = head1[step] - begin
        push = (rate - rate1[step]) * 0.125
        rows = slice(step * 128, (step + 1) * 128)
        kinds = [(shift, change) for shift in SHIFTS_A] + [(shift, push) for shift in SHIFTS_B]
        kinds += [(shift, change) for shift in FAR_A] + [(shift, push) for shift in FAR_B]
        for index, (shift, value) in enumerate(kinds):
            high, low = split(moved(value, shift))
            columns = slice(index * 128, (index + 1) * 128)
            left_high[rows, columns] = high
            left_low[rows, columns] = low

    near_high = left_high[:, : NEAR * 128]
    near_low = left_low[:, : NEAR * 128]
    near = bdot(near_high, near_high_ref[...]) + (
        bdot(near_high, near_low_ref[...]) + bdot(near_low, near_high_ref[...])
    )
    far = bdot(left_high[...], far_ref[...])
    far = far[:, :128] + (far[:, 128:] + bdot(left_low[...], far_ref[:, :128]))
    end_start = power_coarse[0] + 2.0 * power_coarse[1] + power_coarse[2]
    mid_rate_start = power_coarse[1] + power_coarse[2]
    end_rate_start = power_coarse[1] + 2.0 * power_coarse[2] + power_coarse[3]

    ends[0] = begin
    ends_rate[0] = begin_rate
    old_rate, old_twice = begin_rate, begin_twice
    last = power_coarse[1]
    head, rate = begin, begin_rate
    head2[0] = head
    rate2[0] = rate
    tails = []
    for step in range(slices):
        rows = slice(step * 128, (step + 1) * 128)
        tail = near[rows, :128] + end_start
        tail_rate, tail_twice = stage(tail)
        ends[step + 1] = tail
        ends_rate[step + 1] = tail_rate
        next_last = far[rows] + end_rate_start
        integral = (last + 4.0 * (near[rows, 128:] + mid_rate_start) + next_last) * (1.0 / 3.0)
        defect = integral - old_rate
        spread = 0.5 * (old_rate - tail_rate)
        tails.append((defect, defect + spread, old_twice - tail_twice))
        old_rate, old_twice, last = tail_rate, tail_twice, next_last
    for step in range(slices):
        defect, tau, spread_rate = tails[step]
        once, half_twice = stage(rate + defect)
        head, rate = head + rate + tau + 0.5 * once, rate + once + half_twice + spread_rate
        head2[step + 1] = head
        rate2[step + 1] = rate

    previous = jnp.maximum(mine - 1, 0)
    later = jnp.where(mine > 0, 1.0, 0.0).astype(F32)
    table = polynomials()
    parts = {
        "head": head1[mine] - begin,
        "push": (rate1[mine + 1] - rate1[mine]) * 0.125,
        "head_before": (head1[previous] - begin) * later,
        "push_before": (rate1[mine] - rate1[previous]) * (0.125 * later),
        "new_head": head2[mine] - ends[mine],
        "new_push": ((rate2[mine + 1] - ends_rate[mine + 1]) - (rate2[mine] - ends_rate[mine])) * 0.125,
    }
    initial = start[...]
    state = None
    for order in (4, 3, 2, 1, 0):
        total = jnp.zeros((128, 128), F32)
        for name, value in parts.items():
            if table[name][order] != 0.0:
                total = total + table[name][order] * value
        wide = dot3(total, prolong_high_ref[...], prolong_low_ref[...])
        added = jnp.concatenate([wide[:, f * 128 : (f + 1) * 128] for f in range(FIELDS)], axis=0)
        weight = jnp.where(mine > 0, table["later"][order], table["first"][order]).astype(F32)
        added = added + weight * initial
        state = added if state is None else psi(state) + added

    for field in range(FIELDS):
        halves = []
        for index in range(2):
            cos, sin = turning[index]
            begin_row = field * 128 + index * LAYER
            value = state[begin_row : begin_row + LAYER]
            halves.append(value * cos - pltpu.roll(value, 64, 1) * sin)
        even, odd = halves
        real = jnp.where(halved, pltpu.roll(odd, 64, 1), even)
        imaginary = jnp.where(halved, odd, pltpu.roll(even, 64, 1))
        sent_ref[:, field * 128 : (field + 1) * 128] = jnp.where(core == 0, real, imaginary)


IN_VMEM = pl.BlockSpec(memory_space=pltpu.VMEM)


def operators_call(volume_op, lift_op, coarse_volume, coarse_lift, mixing, restrict_op, prolong_op):
    shapes = [
        (256, 256),
        (512, 256),
        (512, 256),
        (FIELDS * 128, 256),
        (128, FIELDS * 128),
        (128, FIELDS * 128),
        (NEAR * 128, 256),
        (NEAR * 128, 256),
        (BLOCKS * 128, 256),
    ]
    return pl.pallas_call(
        operators_kernel,
        out_shape=[jax.ShapeDtypeStruct(shape, BF16) for shape in shapes],
        in_specs=[IN_VMEM] * 7,
        out_specs=[IN_VMEM] * len(shapes),
        compiler_params=pltpu.CompilerParams(vmem_limit_bytes=VMEM_LIMIT),
        cost_estimate=pl.CostEstimate(flops=10**8, bytes_accessed=3 * 10**6, transcendentals=0),
        name="operators",
    )(volume_op, lift_op, coarse_volume, coarse_lift, mixing, restrict_op, prolong_op)


def iterate_kernel_call(slices, received, operators, mixing):
    coarse_shape = pltpu.VMEM((slices + 1, 128, 128), F32)
    return pl.pallas_call(
        functools.partial(iterate_kernel, slices),
        out_shape=jax.ShapeDtypeStruct((LAYER, FIELDS * 128), F32),
        in_specs=[IN_VMEM] * (1 + len(operators)) + [pl.BlockSpec(memory_space=pltpu.SMEM)],
        out_specs=IN_VMEM,
        scratch_shapes=[pltpu.VMEM((FIELDS * 128, 128), F32)]
        + [coarse_shape] * 6
        + [pltpu.VMEM((slices * 128, BLOCKS * 128), BF16)] * 2,
        compiler_params=pltpu.CompilerParams(vmem_limit_bytes=VMEM_LIMIT),
        name="iterate",
    )(received, *operators, mixing)


def iterate_call(slices, received, volume_op, lift_op, coarse_volume, coarse_lift, mixing, restrict_op, prolong_op):
    operators = operators_call(
        volume_op, lift_op, coarse_volume, coarse_lift, mixing, restrict_op, prolong_op
    )
    return iterate_kernel_call(slices, received, operators, mixing)


def on_device(
    initial,
    neighbours,
    volume_op,
    lift_op,
    coarse_volume,
    coarse_lift,
    mixing,
    restrict_op,
    prolong_op,
):
    params = pltpu.CompilerParams(vmem_limit_bytes=VMEM_LIMIT)
    sent, basis = pl.pallas_call(
        to_modes_kernel,
        out_shape=(
            jax.ShapeDtypeStruct((LAYER, (FIELDS + 1) * 128), F32),
            jax.ShapeDtypeStruct((LAYER, 128), F32),
        ),
        in_specs=[IN_VMEM] * 2,
        out_specs=(IN_VMEM, IN_VMEM),
        compiler_params=params,
        name="to_modes",
    )(initial, neighbours)
    arrived = lax.all_to_all(sent[:, None, :], "space", 0, 0, tiled=True)
    pairs = [[i, i + 1] for i in range(0, lax.axis_size("space"), 2)]
    pair = lax.all_gather(arrived, "space", axis_index_groups=pairs)
    received = pair.reshape(2 * LAYER, (FIELDS + 1) * 128)

    operators = operators_call(
        volume_op, lift_op, coarse_volume, coarse_lift, mixing, restrict_op, prolong_op
    )
    modes = iterate_kernel_call(lax.axis_size("tm"), received, operators, mixing)
    returned = lax.all_to_all(modes[:, None, :], "space", 0, 0, tiled=True)
    return pl.pallas_call(
        from_modes_kernel,
        out_shape=jax.ShapeDtypeStruct((1, FIELDS, LAYER, 128), F32),
        in_specs=[IN_VMEM] * 2,
        out_specs=IN_VMEM,
        compiler_params=params,
        name="from_modes",
    )(returned.reshape(LAYER, FIELDS * 128), basis)


def solution(mesh):
    return jax.shard_map(
        on_device,
        mesh=mesh,
        in_specs=(P(None, None, "space"), P(None, "space"), P(), P(), P(), P(), P(), P(), P()),
        out_specs=P("tm", None, None, "space"),
        check_vma=False,
    )
```

```python
import functools

import jax
import jax.numpy as jnp
import numpy as np
from jax import lax
from jax.experimental import pallas as pl
from jax.experimental.pallas import tpu as pltpu
from jax.sharding import PartitionSpec as P

LAYER = 64
FIELDS = 5
DT = 0.125
HALF = 0.7071067811865476
UNITS = 32
STATE = FIELDS * 2 * 128
EDGE = 16
MARGIN = 8
EXACT = lax.Precision.HIGHEST
F32 = jnp.float32
BF16 = jnp.bfloat16
VMEM_LIMIT = 48 * 1024 * 1024


def iota(shape, dim):
    return lax.broadcasted_iota(jnp.int32, shape, dim)


def nn(a, b):
    return lax.dot_general(a, b, (((1,), (0,)), ((), ())), precision=EXACT, preferred_element_type=F32)


def nt(a, b):
    return lax.dot_general(a, b, (((1,), (1,)), ((), ())), precision=EXACT, preferred_element_type=F32)


def nt3(a, b):
    dims = (((1,), (1,)), ((), ()))
    return lax.dot_general(a, b, dims, precision=lax.Precision.HIGH, preferred_element_type=F32)


def eighth_cos(turn):
    turn = turn & 7
    diagonal = jnp.where((turn == 1) | (turn == 7), HALF, jnp.where((turn == 3) | (turn == 5), -HALF, 0.0))
    return jnp.where(turn == 0, 1.0, jnp.where(turn == 4, -1.0, diagonal)).astype(F32)


def wave_numbers(unit):
    low = unit - 23
    high = unit - 26
    kx = jnp.where(unit < 24, unit & 7, jnp.where(unit < 27, low, jnp.where(unit < 30, high, 0)))
    ky = jnp.where(unit < 24, 1 + (unit >> 3), jnp.where(unit < 27, 0, jnp.where(unit == 30, 0, 4)))
    paired = jnp.where(unit < 30, 1, 0)
    kx_other = jnp.where(unit < 30, kx, 4)
    return kx, ky, kx_other, ky, paired


def grid_places(links, base, total, first_slot):
    lane = iota((1, 128), 1)
    upper = lane >= LAYER
    target = iota((128, 128), 0)

    def steps(face):
        one = jnp.where(links[face : face + 1] - base == target, 1.0, 0.0).astype(BF16)
        two = jnp.dot(one, one, preferred_element_type=F32).astype(BF16)
        four = jnp.dot(two, two, preferred_element_type=F32).astype(BF16)
        return one, two, four

    row = iota((8, 128), 0)
    found = jnp.where((row == 0) & ((iota((8, 128), 1) & (LAYER - 1)) == 0), 1.0, 0.0).astype(F32)
    for part, moves in ((1, steps(0)), (2, steps(2))):
        for power, move in enumerate(moves):
            shifted = jnp.dot(found.astype(BF16), move, preferred_element_type=F32)
            found = found + shifted + jnp.where(row == part, shifted[0:1] * (1 << power), 0.0)
    along_x = found[1:2]
    along_y = found[2:3]

    below = jnp.where(upper, base, (base + total - LAYER) % total)
    hit = links[4:5] == below
    extra = jnp.zeros((1, 128), F32)
    for slot, (layer_upper, value) in enumerate(
        ((False, along_x), (False, along_y), (True, along_x), (True, along_y))
    ):
        part = jnp.where(hit & (upper == layer_upper), value, 0.0)
        extra = jnp.where(lane == first_slot + slot, jnp.sum(part, axis=1, keepdims=True), extra)
    return along_x.astype(jnp.int32), along_y.astype(jnp.int32), extra


def layer_modes(ref, where, places, first_slot):
    upper = iota((1, 128), 1) >= LAYER
    halved = iota((UNITS, 128), 1) >= LAYER
    mode = iota((LAYER, 128), 0)
    kx, ky, kx_other, ky_other, paired = wave_numbers(mode & (UNITS - 1))
    second = mode >= UNITS
    links = ref[FIELDS * LAYER :].astype(jnp.int32)
    along_x, along_y, extra = grid_places(links, where * 2 * LAYER, places * 2 * LAYER, first_slot)
    turns = jnp.where(second, kx_other, kx) * along_x + jnp.where(second, ky_other, ky) * along_y
    basis = eighth_cos(turns + jnp.where(second, 2 * paired, 0))
    apart = jnp.concatenate([jnp.where(upper, 0.0, basis), jnp.where(upper, basis, 0.0)], axis=0)

    def of_field(field):
        state = ref[field * LAYER : (field + 1) * LAYER]
        modes = nt3(apart, jnp.concatenate([state, state], axis=0))
        return [
            jnp.where(
                halved,
                modes[index * LAYER + UNITS : (index + 1) * LAYER],
                modes[index * LAYER : index * LAYER + UNITS],
            )
            for index in range(2)
        ]

    return basis, of_field, extra


def own_modes_kernel(own_ref, modes_ref, basis_ref):
    basis, of_field, extra = layer_modes(own_ref, lax.axis_index("space"), lax.axis_size("space"), 0)
    basis_ref[...] = basis
    for field in range(FIELDS):
        for index, value in enumerate(of_field(field)):
            column = (field * 2 + index) * 128
            modes_ref[:, column : column + 128] = value
    modes_ref[:, STATE:] = jnp.broadcast_to(extra, (UNITS, 128))


def both_modes_kernel(own_ref, beside_ref, sent_ref, blocks, semaphores):
    place = lax.axis_index("space")
    places = lax.axis_size("space")
    partner = (jnp.where(((place >> 3) & 3) < 2, place - EDGE, place + EDGE) + places) % places
    for column in range(0, STATE, 128):
        blocks[:, 0, column : column + 128] = own_ref[:, column : column + 128]
    first = pltpu.make_async_copy(blocks.at[:, :, :STATE], sent_ref.at[:, :, :STATE], semaphores.at[0])
    first.start()
    _, of_field, extra = layer_modes(beside_ref, partner, places, 4)
    for field in range(FIELDS):
        for index, value in enumerate(of_field(field)):
            column = STATE + (field * 2 + index) * 128
            blocks[:, 0, column : column + 128] = value
    blocks[:, 0, 2 * STATE :] = own_ref[:, STATE:] + jnp.broadcast_to(extra, (UNITS, 128))
    second = pltpu.make_async_copy(blocks.at[:, :, STATE:], sent_ref.at[:, :, STATE:], semaphores.at[1])
    second.start()
    first.wait()
    second.wait()


def from_modes_kernel(modes_ref, basis_ref, out_ref):
    unit = iota((LAYER, 128), 0) & (UNITS - 1)
    scale = jnp.where(unit < 30, 2.0 / LAYER, 1.0 / LAYER).astype(F32)
    back = basis_ref[...] * scale
    upper = iota((LAYER, 128), 1) >= LAYER
    halved = iota((UNITS, 128), 1) >= LAYER
    for field in range(FIELDS):
        column = field * 256
        even = modes_ref[:, 0, column : column + 128]
        odd = modes_ref[:, 0, column + 128 : column + 256]
        real = jnp.where(halved, pltpu.roll(odd, 64, 1), even)
        imaginary = jnp.where(halved, odd, pltpu.roll(even, 64, 1))
        whole = nn(jnp.transpose(jnp.concatenate([real, imaginary], axis=0)), back)
        out_ref[0, field] = jnp.where(upper, whole[LAYER:], whole[:LAYER])


SHIFTS_A = (0, 1, -1, 2, -2)
SHIFTS_B = (0, 1, -1)
FAR_A = (3, -3)
FAR_B = (2, -2)
NEAR = len(SHIFTS_A) + len(SHIFTS_B)
BLOCKS = NEAR + len(FAR_A) + len(FAR_B)
RING = 8


def face_weights(shape, per_edge, node, weights):
    column = iota(shape, 1)
    face = column // (per_edge * per_edge)
    trace = column % (per_edge * per_edge)
    a, b, c = (node // (per_edge * per_edge), (node // per_edge) % per_edge, node % per_edge)
    first = [a, a, b, b, c, c]
    rest = [b * per_edge + c] * 2 + [a * per_edge + c] * 2 + [a * per_edge + b] * 2
    result = jnp.zeros(shape, F32)
    for which, weight in weights.items():
        edge = per_edge - 1 if which % 2 == 0 else 0
        on = (face == which) & (first[which] == edge) & (rest[which] == trace)
        result = jnp.where(on, weight, result)
    return result


def split(value):
    high = value.astype(BF16)
    return high, (value - high.astype(F32)).astype(BF16)


def bdot(a, b):
    return jnp.dot(a, b, preferred_element_type=F32)


def operators_kernel(
    volume_ref,
    lift_ref,
    coarse_volume_ref,
    coarse_lift_ref,
    mixing_ref,
    restrict_ref,
    prolong_ref,
    fine_ref,
    chain_high_ref,
    chain_low_ref,
    restrict_all_ref,
    prolong_high_ref,
    prolong_low_ref,
    near_high_ref,
    near_low_ref,
    far_ref,
    *scratch,
):
    *held, semaphores = scratch
    operands = (
        volume_ref,
        lift_ref,
        coarse_volume_ref,
        coarse_lift_ref,
        mixing_ref,
        restrict_ref,
        prolong_ref,
    )
    copies = [
        pltpu.make_async_copy(operand, place_for, semaphores.at[index])
        for index, (operand, place_for) in enumerate(zip(operands, held))
    ]
    for copy in copies:
        copy.start()
    for copy in copies:
        copy.wait()
    volume_ref, lift_ref, coarse_volume_ref, coarse_lift_ref, mixing_ref, restrict_ref, prolong_ref = held
    place = lax.axis_index("space")
    kx, ky, kx_other, ky_other, paired = wave_numbers(place & (UNITS - 1))
    single = paired == 0

    def turn_cos(first, second, second_half):
        return jnp.where(second_half, eighth_cos(second), eighth_cos(first))

    def put_packed(ref, rows, value):
        high, low = split(value)
        ref[rows, :128] = high
        ref[rows, 128:] = low

    def put(high_ref, low_ref, rows, columns, value):
        high, low = split(value)
        high_ref[rows, columns] = high
        low_ref[rows, columns] = low

    wide = iota((128, 128), 1)
    tall = iota((128, 128), 0)
    row = iota((128, 96), 0)
    half = row >= 64
    same = (wide >= 64) == (tall >= 64)
    cos_x = turn_cos(kx, kx_other, half)
    cos_y = turn_cos(ky, ky_other, half)
    sin_x = jnp.where(single, 0.0, eighth_cos(kx - 2))
    sin_y = jnp.where(single, 0.0, eighth_cos(ky - 2))
    sign = jnp.where(half, -1.0, 1.0)
    along = face_weights((128, 96), 4, row & 63, {0: cos_x, 1: cos_x, 2: cos_y, 3: cos_y})
    across = face_weights(
        (128, 96), 4, row & 63, {0: -sin_x * sign, 1: sin_x * sign, 2: -sin_y * sign, 3: sin_y * sign}
    )
    ahead = face_weights((128, 96), 4, row & 63, {4: 1.0, 5: 1.0})
    lift2 = jnp.concatenate([lift_ref[...]] * 2, axis=0)
    volume2 = jnp.concatenate([volume_ref[...]] * 2, axis=0)
    twice = jnp.where((iota((128, 64), 0) & 63) == iota((128, 64), 1), 1.0, 0.0).astype(F32)
    inside = (DT / 2) * jnp.where(same, nt(twice, volume2) + nt(along, lift2), nt(across, lift2))
    beside = (DT / 2) * jnp.where(same, nt(ahead, lift2), 0.0)
    put_packed(fine_ref, slice(0, 128), inside)
    put_packed(fine_ref, slice(128, 256), beside)
    psi = jnp.concatenate([inside, beside], axis=0)

    row = iota((128, 24), 0)
    half = ((row >> 3) & 1) == 1
    cos_x = turn_cos(kx, kx_other, half)
    cos_y = turn_cos(ky, ky_other, half)
    sign = jnp.where(half, -1.0, 1.0)
    along = face_weights((128, 24), 2, row & 7, {0: cos_x, 1: cos_x, 2: cos_y, 3: cos_y})
    across = face_weights(
        (128, 24), 2, row & 7, {0: -sin_x * sign, 1: sin_x * sign, 2: -sin_y * sign, 3: sin_y * sign}
    )
    ahead = face_weights((128, 24), 2, row & 7, {4: 1.0, 5: 1.0})
    node8 = jnp.where((iota((128, 8), 0) & 7) == iota((128, 8), 1), 1.0, 0.0).astype(F32)
    field8 = jnp.where((iota((128, FIELDS), 0) >> 4) == iota((128, FIELDS), 1), 1.0, 0.0).astype(F32)
    same = ((wide >> 3) & 1) == ((tall >> 3) & 1)
    clift = coarse_lift_ref[...]
    mixing = mixing_ref[...]
    power = nt(field8, mixing)
    coupled = [nt(field8, field8), nt(power, field8)]
    for _ in range(2):
        power = nt(power, mixing)
        coupled.append(nt(power, field8))
    along = nt(nt(node8, coarse_volume_ref[...]) + nt(along, clift), node8)
    across = nt(nt(across, clift), node8)
    ahead = nt(nt(ahead, clift), node8)
    level = DT * coupled[1] * jnp.where(same, along, across)
    beside = DT * coupled[1] * jnp.where(same, ahead, 0.0)
    upper = (tall & 1) == 1
    below = jnp.where(upper, beside, 0.0)
    above = jnp.where(upper, 0.0, beside)
    level_level = nn(level, level)
    below_all = nn(below, jnp.concatenate([level, below, above], axis=1))
    above_all = nn(above, jnp.concatenate([level, below, above], axis=1))
    once = [level, below, above, jnp.zeros((128, 128), F32)]
    squared = [
        level_level + below_all[:, 256:] + above_all[:, 128:256],
        nn(level, below) + below_all[:, :128],
        nn(level, above) + above_all[:, :128],
        below_all[:, 128:256] + above_all[:, 256:],
    ]
    for block in range(4):
        rows = slice(block * 128, (block + 1) * 128)
        put(chain_high_ref, chain_low_ref, rows, slice(0, 128), once[block])
        put(chain_high_ref, chain_low_ref, rows, slice(128, 256), 0.5 * squared[block])

    restricting = nt(twice, nn(node8, restrict_ref[...]))
    prolonging = nt(node8, jnp.concatenate([prolong_ref[...]] * 2, axis=0))
    down = (tall >= 64) == (((wide >> 3) & 1) == 1)
    up = (wide >= 64) == (((tall >> 3) & 1) == 1)
    restricting = jnp.where(down, restricting, 0.0)
    prolonging = jnp.where(up, prolonging, 0.0)
    for field in range(FIELDS):
        part = slice(field * 128, (field + 1) * 128)
        put_packed(restrict_all_ref, part, jnp.where((wide >> 4) == field, restricting, 0.0))
        put(prolong_high_ref, prolong_low_ref, slice(0, 128), part, jnp.where((tall >> 4) == field, prolonging, 0.0))

    response = jnp.where(tall < 16, prolonging, 0.0)
    fine_below = (wide & 3) == 3
    responses = [nn(response, restricting)]
    for _ in range(3):
        near = jnp.where(fine_below, pltpu.roll(response, 16, 0), pltpu.roll(response, 112, 0))
        response = nn(jnp.concatenate([response, near], axis=1), psi)
        responses.append(nn(response, restricting))

    def block(shift, weights):
        rows = slice((shift % RING) * 16, (shift % RING) * 16 + 16)
        total = jnp.zeros((128, 128), F32)
        for order, weight in weights.items():
            if abs(shift) <= order:
                total = total + weight * coupled[order] * jnp.concatenate([responses[order][rows]] * 8, axis=0)
        return total

    kinds = [(shift, 0) for shift in SHIFTS_A] + [(shift, 1) for shift in SHIFTS_B]
    kinds += [(shift, 0) for shift in FAR_A] + [(shift, 1) for shift in FAR_B]
    ends = ({0: 1.0, 1: 2.0, 2: 1.0}, {0: 2.0, 1: 1.0})
    mid_rates = ({1: 1.0, 2: 1.0}, {1: 1.0})
    end_rates = ({1: 1.0, 2: 2.0, 3: 1.0}, {1: 2.0, 2: 1.0})
    for index, (shift, kind) in enumerate(kinds):
        rows = slice(index * 128, (index + 1) * 128)
        if index < NEAR:
            put(near_high_ref, near_low_ref, rows, slice(0, 128), block(shift, ends[kind]))
            put(near_high_ref, near_low_ref, rows, slice(128, 256), block(shift, mid_rates[kind]))
        put_packed(far_ref, rows, block(shift, end_rates[kind]))


def shifted(even, odd, shift):
    def rolled(value, by):
        return value if by == 0 else pltpu.roll(value, by % len(value), 0)

    if shift % 2 == 0:
        return rolled(even, shift // 2), rolled(odd, shift // 2)
    return rolled(odd, (shift + 1) // 2), rolled(even, (shift - 1) // 2)


def beside_layers(state, from_below, reach=1):
    half = len(state) // 2
    even, odd = state[:half], state[half:]
    below = shifted(even, odd, reach)
    above = shifted(even, odd, -reach)
    return jnp.concatenate([jnp.where(from_below, low, high) for low, high in zip(below, above)], axis=0)


def moved(state, shift):
    return jnp.concatenate(shifted(state[:LAYER], state[LAYER:], shift), axis=0)


def polynomials():
    once = np.array([1.0, 1.0])
    twice = np.polymul(once, once)
    two = np.array([1.0, 2.0])
    on_start = np.array([5 / 12, 4 / 3, 1.0])
    on_mid = np.array([2 / 3, 1 / 3, 0.0])
    on_end = np.array([-1 / 12, 1 / 3, 0.0])
    own = np.polyadd(np.polymul(on_mid, once), np.polymul(on_end, twice))
    table = {
        "first": np.polyadd(on_start, own),
        "later": np.polyadd(np.polymul(on_start, twice), own),
        "head": own,
        "push": np.polyadd(on_mid, np.polymul(on_end, two)),
        "head_before": np.polymul(on_start, twice),
        "push_before": np.polymul(on_start, two),
        "new_head": twice,
        "new_push": two,
    }
    return {name: [float(x) for x in np.pad(p[::-1], (0, 5 - len(p)))] for name, p in table.items()}


def iterate_kernel(
    slices,
    received_ref,
    fine_ref,
    chain_high_ref,
    chain_low_ref,
    restrict_all_ref,
    prolong_high_ref,
    prolong_low_ref,
    near_high_ref,
    near_low_ref,
    far_ref,
    mixing_ref,
    sent_ref,
    start,
    head1,
    rate1,
    head2,
    rate2,
    ends,
    ends_rate,
    mixing_smem,
    semaphore,
):
    fetch = pltpu.make_async_copy(mixing_ref, mixing_smem, semaphore)
    fetch.start()
    place = lax.axis_index("space")
    mine = lax.axis_index("tm")
    kx, ky, kx_other, ky_other, paired = wave_numbers(place & (UNITS - 1))
    single = paired == 0
    lane = iota((LAYER, 128), 1)
    fine_below = (lane & 3) == 3
    coarse_below = (lane & 1) == 1
    halved = lane >= 64

    def packed_dot(value, packed):
        high, low = split(value)
        both = bdot(high, packed)
        return both[:, :128] + (both[:, 128:] + bdot(low, packed[:, :128]))

    def dot3(value, high_op, low_op):
        high, low = split(value)
        return bdot(high, high_op) + (bdot(high, low_op) + bdot(low, high_op))

    def fields_of(state):
        rows = len(state) // FIELDS
        return [state[field * rows : (field + 1) * rows] for field in range(FIELDS)]

    def psi(state):
        parts = fields_of(state)
        pieces = []
        for field in range(FIELDS):
            mixed = mixing_smem[field, 0] * parts[0]
            for other in range(1, FIELDS):
                mixed = mixed + mixing_smem[field, other] * parts[other]
            pieces.append(jnp.concatenate([mixed, beside_layers(mixed, fine_below[: len(mixed) // 2])], axis=1))
        return packed_dot(jnp.concatenate(pieces, axis=0), fine_ref[...])

    def restrict(state):
        return packed_dot(jnp.concatenate(fields_of(state), axis=1), restrict_all_ref[...])

    def stages(states):
        wide = [
            jnp.concatenate(
                [state, moved(state, 1), moved(state, -1), beside_layers(state, coarse_below, 2)], axis=1
            )
            for state in states
        ]
        both = dot3(jnp.concatenate(wide, axis=0), chain_high_ref[...], chain_low_ref[...])
        both = [both[i * 128 : (i + 1) * 128] for i in range(len(states))]
        return [(part[:, :128], part[:, 128:]) for part in both]

    def in_order(column):
        begin = column if column < STATE else 2 * STATE
        own = received_ref[:, 0, begin : begin + 128]
        if column < STATE:
            other = received_ref[:, 0, STATE + column : STATE + column + 128]
        else:
            other = pltpu.roll(own, 124, 1)
        return jnp.concatenate([other[:EDGE], own, other[EDGE:]], axis=0)

    shifts = in_order(STATE)
    lower_triangle = jnp.where(iota((LAYER, LAYER), 1) < iota((LAYER, LAYER), 0), 1.0, 0.0).astype(F32)
    first_x, first_y = shifts[:, 0:1], shifts[:, 1:2]
    both_x, both_y = first_x + shifts[:, 2:3], first_y + shifts[:, 3:4]
    passed_x = nn(lower_triangle, jnp.broadcast_to(both_x, (LAYER, 128)))
    passed_y = nn(lower_triangle, jnp.broadcast_to(both_y, (LAYER, 128)))
    turning = []
    for add_x, add_y in ((first_x, first_y), (both_x, both_y)):
        shift_x = (passed_x + add_x).astype(jnp.int32)
        shift_y = (passed_y + add_y).astype(jnp.int32)
        turns = jnp.where(halved, kx_other, kx) * shift_x + jnp.where(halved, ky_other, ky) * shift_y
        cos = eighth_cos(turns)
        sin = jnp.where(single, 0.0, eighth_cos(turns - 2))
        turning.append((cos, jnp.where(halved, sin, -sin)))

    for field in range(FIELDS):
        for index in range(2):
            value = in_order((field * 2 + index) * 128)
            cos, sin = turning[index]
            begin = field * 128 + index * LAYER
            start[begin : begin + LAYER] = value * cos + pltpu.roll(value, 64, 1) * sin

    fetch.wait()

    initial = start[...]
    power = psi(initial)
    begin = restrict(initial)
    power_coarse = [begin, restrict(power)]
    ((begin_rate, begin_twice),) = stages([begin])
    defect = 2.0 * power_coarse[1] - begin_rate
    head, rate = begin, begin_rate
    later_head, later_rate = begin, begin_rate
    old_rate, old_twice, last = begin_rate, begin_twice, power_coarse[1]
    head1[0], rate1[0] = begin, begin_rate
    head2[0], rate2[0] = begin, begin_rate
    ends[0], ends_rate[0] = begin, begin_rate

    def needed(change, push):
        kinds = [(shift, change) for shift in SHIFTS_A] + [(shift, push) for shift in SHIFTS_B]
        kinds += [(shift, change) for shift in FAR_A] + [(shift, push) for shift in FAR_B]
        parts = [split(moved(value, shift)) for shift, value in kinds]
        high = jnp.concatenate([part[0] for part in parts], axis=1)
        low = jnp.concatenate([part[1] for part in parts], axis=1)
        near_high, near_low = high[:, : NEAR * 128], low[:, : NEAR * 128]
        near = bdot(near_high, near_high_ref[...]) + (
            bdot(near_high, near_low_ref[...]) + bdot(near_low, near_high_ref[...])
        )
        far = bdot(high, far_ref[...])
        return near[:, :128], near[:, 128:], far[:, :128] + (far[:, 128:] + bdot(low, far_ref[:, :128]))

    previous = jnp.maximum(mine - 1, 0)
    later = jnp.where(mine > 0, 1.0, 0.0).astype(F32)
    table = polynomials()

    def around(state):
        half = len(state) // 2
        return jnp.concatenate(
            [state[EDGE - MARGIN : EDGE + UNITS + MARGIN], state[half + EDGE - MARGIN : half + EDGE + UNITS + MARGIN]],
            axis=0,
        )

    initial_around = jnp.concatenate([around(part) for part in fields_of(initial)], axis=0)

    def added(order):
        total = None
        for name, value in parts.items():
            if table[name][order] != 0.0:
                term = table[name][order] * value
                total = term if total is None else total + term
        wide = dot3(total, prolong_high_ref[...], prolong_low_ref[...])
        wide = jnp.concatenate([wide[:, f * 128 : (f + 1) * 128] for f in range(FIELDS)], axis=0)
        weight = jnp.where(mine > 0, table["later"][order], table["first"][order]).astype(F32)
        return wide + weight * initial_around

    waiting = []
    ready = None
    for step in range(slices + 2):
        states = []
        if step < slices:
            states.append(rate + defect)
        if ready is not None:
            tail = ready[0] + end_start
            next_last = ready[2] + end_rate_start
            integral = (last + 4.0 * (ready[1] + mid_rate_start) + next_last) * (1.0 / 3.0)
            later_defect = integral - old_rate
            states += [tail, later_rate + later_defect]
        found = stages(states)
        if ready is not None:
            (tail_rate, tail_twice), (once, half_twice) = found[-2:]
            later_head = later_head + later_rate + later_defect + 0.5 * (old_rate - tail_rate + once)
            later_rate = later_rate + once + half_twice + (old_twice - tail_twice)
            old_rate, old_twice, last = tail_rate, tail_twice, next_last
            slot = step - 1
            head2[slot], rate2[slot] = later_head, later_rate
            ends[slot], ends_rate[slot] = tail, tail_rate
        ready = needed(*waiting.pop()) if waiting else None
        if step < slices:
            once, half_twice = found[0]
            change = head - begin
            head, next_rate = head + rate + defect + 0.5 * once, rate + once + half_twice
            waiting.append((change, (next_rate - rate) * 0.125))
            rate = next_rate
            head1[step + 1], rate1[step + 1] = head, rate
        if step == slices - 1:
            parts = {
                "head": around(head1[mine] - begin),
                "push": around((rate1[mine + 1] - rate1[mine]) * 0.125),
                "head_before": around((head1[previous] - begin) * later),
                "push_before": around((rate1[mine] - rate1[previous]) * (0.125 * later)),
            }
            state = added(4)
            state = psi(state) + added(3)
        if step < 2:
            power = psi(power)
            power_coarse.append(restrict(power))
        if step == 1:
            end_start = power_coarse[0] + 2.0 * power_coarse[1] + power_coarse[2]
            mid_rate_start = power_coarse[1] + power_coarse[2]
            end_rate_start = power_coarse[1] + 2.0 * power_coarse[2] + power_coarse[3]

    new_head = head2[mine] - ends[mine]
    new_push = ((rate2[mine + 1] - ends_rate[mine + 1]) - (rate2[mine] - ends_rate[mine])) * 0.125
    parts["new_head"], parts["new_push"] = around(new_head), around(new_push)
    for order in (2, 1, 0):
        state = psi(state) + added(order)
    turned = [(cos[EDGE - MARGIN : EDGE + UNITS + MARGIN], sin[EDGE - MARGIN : EDGE + UNITS + MARGIN]) for cos, sin in turning]
    rows = len(state) // (2 * FIELDS)
    for field in range(FIELDS):
        for index in range(2):
            cos, sin = turned[index]
            begin_row = (field * 2 + index) * rows
            value = state[begin_row : begin_row + rows]
            value = value * cos - pltpu.roll(value, 64, 1) * sin
            column = (field * 2 + index) * 128
            sent_ref[:, 0, column : column + 128] = value[MARGIN : MARGIN + UNITS]


IN_VMEM = pl.BlockSpec(memory_space=pltpu.VMEM)
ANYWHERE = pl.BlockSpec(memory_space=pltpu.HBM)


def operators_call(volume_op, lift_op, coarse_volume, coarse_lift, mixing, restrict_op, prolong_op):
    shapes = [
        (256, 256),
        (512, 256),
        (512, 256),
        (FIELDS * 128, 256),
        (128, FIELDS * 128),
        (128, FIELDS * 128),
        (NEAR * 128, 256),
        (NEAR * 128, 256),
        (BLOCKS * 128, 256),
    ]
    return pl.pallas_call(
        operators_kernel,
        out_shape=[jax.ShapeDtypeStruct(shape, BF16) for shape in shapes],
        in_specs=[ANYWHERE] * 7,
        out_specs=[IN_VMEM] * len(shapes),
        scratch_shapes=[
            pltpu.VMEM(operand.shape, F32)
            for operand in (volume_op, lift_op, coarse_volume, coarse_lift, mixing, restrict_op, prolong_op)
        ]
        + [pltpu.SemaphoreType.DMA((7,))],
        compiler_params=pltpu.CompilerParams(vmem_limit_bytes=VMEM_LIMIT),
        cost_estimate=pl.CostEstimate(flops=10**8, bytes_accessed=3 * 10**6, transcendentals=0),
        name="operators",
    )(volume_op, lift_op, coarse_volume, coarse_lift, mixing, restrict_op, prolong_op)


def iterate_kernel_call(slices, received, operators, mixing):
    coarse_shape = pltpu.VMEM((slices + 1, 128, 128), F32)
    return pl.pallas_call(
        functools.partial(iterate_kernel, slices),
        out_shape=jax.ShapeDtypeStruct((UNITS, 1, STATE), F32),
        in_specs=[IN_VMEM] * (1 + len(operators)) + [ANYWHERE],
        out_specs=IN_VMEM,
        scratch_shapes=[pltpu.VMEM((FIELDS * 128, 128), F32)]
        + [coarse_shape] * 6
        + [pltpu.SMEM((FIELDS, FIELDS), F32), pltpu.SemaphoreType.DMA],
        compiler_params=pltpu.CompilerParams(vmem_limit_bytes=VMEM_LIMIT),
        name="iterate",
    )(received, *operators, mixing)


def iterate_call(slices, received, volume_op, lift_op, coarse_volume, coarse_lift, mixing, restrict_op, prolong_op):
    operators = operators_call(
        volume_op, lift_op, coarse_volume, coarse_lift, mixing, restrict_op, prolong_op
    )
    return iterate_kernel_call(slices, received[:, None, :], operators, mixing)


def window_partners(slices, places):
    per_chip_row = 8
    depth = places // per_chip_row
    ring = 2 * depth
    route = []
    for slot in range(slices):
        for place in range(places):
            z = slot % 2 * depth + place // per_chip_row
            other = (z - 2 if z % 4 < 2 else z + 2) % ring
            partner = (slot - slot % 2 + other // depth) * places + other % depth * per_chip_row
            route.append((partner + place % per_chip_row, slot * places + place))
    return route


def on_device(
    initial,
    neighbours,
    volume_op,
    lift_op,
    coarse_volume,
    coarse_lift,
    mixing,
    restrict_op,
    prolong_op,
):
    params = pltpu.CompilerParams(vmem_limit_bytes=VMEM_LIMIT)
    rows = FIELDS * LAYER
    own = jnp.pad(initial.reshape(rows, -1), ((0, len(neighbours)), (0, 0)))
    own = own + jnp.pad(neighbours, ((rows, 0), (0, 0))).astype(F32)
    beside = lax.ppermute(own, ("tm", "space"), window_partners(lax.axis_size("tm"), lax.axis_size("space")))
    modes, basis = pl.pallas_call(
        own_modes_kernel,
        out_shape=(
            jax.ShapeDtypeStruct((UNITS, STATE + 128), F32),
            jax.ShapeDtypeStruct((LAYER, 128), F32),
        ),
        in_specs=[IN_VMEM],
        out_specs=(IN_VMEM, IN_VMEM),
        compiler_params=params,
        name="own_modes",
    )(own)
    sent = pl.pallas_call(
        both_modes_kernel,
        out_shape=jax.ShapeDtypeStruct((UNITS, 1, 2 * STATE + 128), F32),
        in_specs=[IN_VMEM] * 2,
        out_specs=pl.BlockSpec(memory_space=pl.ANY),
        scratch_shapes=[
            pltpu.VMEM((UNITS, 1, 2 * STATE + 128), F32),
            pltpu.SemaphoreType.DMA((2,)),
        ],
        compiler_params=params,
        name="both_modes",
    )(modes, beside)
    windows = [[first + i for i in range(UNITS)] for first in range(0, lax.axis_size("space"), UNITS)]

    def exchange(blocks):
        return lax.all_to_all(blocks, "space", 0, 0, axis_index_groups=windows, tiled=True)

    received = exchange(sent)
    operators = operators_call(
        volume_op, lift_op, coarse_volume, coarse_lift, mixing, restrict_op, prolong_op
    )
    modes = iterate_kernel_call(lax.axis_size("tm"), received, operators, mixing)
    returned = exchange(modes)
    return pl.pallas_call(
        from_modes_kernel,
        out_shape=jax.ShapeDtypeStruct((1, FIELDS, LAYER, 128), F32),
        in_specs=[IN_VMEM] * 2,
        out_specs=IN_VMEM,
        compiler_params=params,
        name="from_modes",
    )(returned, basis)


def solution(mesh):
    return jax.shard_map(
        on_device,
        mesh=mesh,
        in_specs=(P(None, None, "space"), P(None, "space"), P(), P(), P(), P(), P(), P(), P()),
        out_specs=P("tm", None, None, "space"),
        check_vma=False,
    )
```

```python
import functools

import jax
import jax.numpy as jnp
import numpy as np
from jax import lax
from jax.experimental import pallas as pl
from jax.experimental.pallas import tpu as pltpu
from jax.sharding import PartitionSpec as P

LAYER = 64
FIELDS = 5
DT = 0.125
HALF = 0.7071067811865476
UNITS = 32
STATE = FIELDS * 2 * 128
EDGE = 16
MARGIN = 8
EXACT = lax.Precision.HIGHEST
F32 = jnp.float32
BF16 = jnp.bfloat16
VMEM_LIMIT = 20 * 1024 * 1024


def iota(shape, dim):
    return lax.broadcasted_iota(jnp.int32, shape, dim)


def nn(a, b):
    return lax.dot_general(a, b, (((1,), (0,)), ((), ())), precision=EXACT, preferred_element_type=F32)


def nt(a, b):
    return lax.dot_general(a, b, (((1,), (1,)), ((), ())), precision=EXACT, preferred_element_type=F32)


def nt3(a, b):
    dims = (((1,), (1,)), ((), ()))
    return lax.dot_general(a, b, dims, precision=lax.Precision.HIGH, preferred_element_type=F32)


def eighth_cos(turn):
    turn = turn & 7
    diagonal = jnp.where((turn == 1) | (turn == 7), HALF, jnp.where((turn == 3) | (turn == 5), -HALF, 0.0))
    return jnp.where(turn == 0, 1.0, jnp.where(turn == 4, -1.0, diagonal)).astype(F32)


def wave_numbers(unit):
    low = unit - 23
    high = unit - 26
    kx = jnp.where(unit < 24, unit & 7, jnp.where(unit < 27, low, jnp.where(unit < 30, high, 0)))
    ky = jnp.where(unit < 24, 1 + (unit >> 3), jnp.where(unit < 27, 0, jnp.where(unit == 30, 0, 4)))
    paired = jnp.where(unit < 30, 1, 0)
    kx_other = jnp.where(unit < 30, kx, 4)
    return kx, ky, kx_other, ky, paired


def grid_places(links, base, total, first_slot):
    lane = iota((1, 128), 1)
    upper = lane >= LAYER
    target = iota((128, 128), 0)

    def steps(face):
        one = jnp.where(links[face : face + 1] - base == target, 1.0, 0.0).astype(BF16)
        two = jnp.dot(one, one, preferred_element_type=F32).astype(BF16)
        four = jnp.dot(two, two, preferred_element_type=F32).astype(BF16)
        return one, two, four

    row = iota((8, 128), 0)
    found = jnp.where((row == 0) & ((iota((8, 128), 1) & (LAYER - 1)) == 0), 1.0, 0.0).astype(F32)
    for part, moves in ((1, steps(0)), (2, steps(2))):
        for power, move in enumerate(moves):
            shifted = jnp.dot(found.astype(BF16), move, preferred_element_type=F32)
            found = found + shifted + jnp.where(row == part, shifted[0:1] * (1 << power), 0.0)
    along_x = found[1:2]
    along_y = found[2:3]

    below = jnp.where(upper, base, (base + total - LAYER) % total)
    hit = links[4:5] == below
    extra = jnp.zeros((1, 128), F32)
    for slot, (layer_upper, value) in enumerate(
        ((False, along_x), (False, along_y), (True, along_x), (True, along_y))
    ):
        part = jnp.where(hit & (upper == layer_upper), value, 0.0)
        extra = jnp.where(lane == first_slot + slot, jnp.sum(part, axis=1, keepdims=True), extra)
    return along_x.astype(jnp.int32), along_y.astype(jnp.int32), extra


def layer_modes(ref, links, where, places, first_slot):
    upper = iota((1, 128), 1) >= LAYER
    halved = iota((UNITS, 128), 1) >= LAYER
    mode = iota((LAYER, 128), 0)
    kx, ky, kx_other, ky_other, paired = wave_numbers(mode & (UNITS - 1))
    second = mode >= UNITS
    along_x, along_y, extra = grid_places(links, where * 2 * LAYER, places * 2 * LAYER, first_slot)
    turns = jnp.where(second, kx_other, kx) * along_x + jnp.where(second, ky_other, ky) * along_y
    basis = eighth_cos(turns + jnp.where(second, 2 * paired, 0))
    apart = jnp.concatenate([jnp.where(upper, 0.0, basis), jnp.where(upper, basis, 0.0)], axis=0)

    def of_field(field):
        state = ref[field * LAYER : (field + 1) * LAYER]
        modes = nt3(apart, jnp.concatenate([state, state], axis=0))
        return [
            jnp.where(
                halved,
                modes[index * LAYER + UNITS : (index + 1) * LAYER],
                modes[index * LAYER : index * LAYER + UNITS],
            )
            for index in range(2)
        ]

    return basis, of_field, extra


def own_modes_kernel(own_ref, links_ref, modes_ref, basis_ref):
    basis, of_field, extra = layer_modes(own_ref, links_ref[...], lax.axis_index("space"), lax.axis_size("space"), 0)
    basis_ref[...] = basis
    for field in range(FIELDS):
        for index, value in enumerate(of_field(field)):
            column = (field * 2 + index) * 128
            modes_ref[:, column : column + 128] = value
    modes_ref[:, STATE:] = jnp.broadcast_to(extra, (UNITS, 128))


def both_modes_kernel(own_ref, beside_ref, links_ref, sent_ref, blocks, semaphores):
    place = lax.axis_index("space")
    places = lax.axis_size("space")
    partner = (jnp.where(((place >> 3) & 3) < 2, place - EDGE, place + EDGE) + places) % places
    for column in range(0, STATE, 128):
        blocks[:, 0, column : column + 128] = own_ref[:, column : column + 128]
    first = pltpu.make_async_copy(blocks.at[:, :, :STATE], sent_ref.at[:, :, :STATE], semaphores.at[0])
    first.start()
    _, of_field, extra = layer_modes(beside_ref, links_ref[...], partner, places, 4)
    for field in range(FIELDS):
        for index, value in enumerate(of_field(field)):
            column = STATE + (field * 2 + index) * 128
            blocks[:, 0, column : column + 128] = value
    blocks[:, 0, 2 * STATE :] = own_ref[:, STATE:] + jnp.broadcast_to(extra, (UNITS, 128))
    second = pltpu.make_async_copy(blocks.at[:, :, STATE:], sent_ref.at[:, :, STATE:], semaphores.at[1])
    second.start()
    first.wait()
    second.wait()


def from_modes_kernel(modes_ref, basis_ref, out_ref, fields, semaphores):
    copies = []
    unit = iota((LAYER, 128), 0) & (UNITS - 1)
    scale = jnp.where(unit < 30, 2.0 / LAYER, 1.0 / LAYER).astype(F32)
    back = basis_ref[...] * scale
    upper = iota((LAYER, 128), 1) >= LAYER
    halved = iota((UNITS, 128), 1) >= LAYER
    for field in range(FIELDS):
        column = field * 256
        even = modes_ref[:, 0, column : column + 128]
        odd = modes_ref[:, 0, column + 128 : column + 256]
        real = jnp.where(halved, pltpu.roll(odd, 64, 1), even)
        imaginary = jnp.where(halved, odd, pltpu.roll(even, 64, 1))
        whole = nn(jnp.transpose(jnp.concatenate([real, imaginary], axis=0)), back)
        fields[field] = jnp.where(upper, whole[LAYER:], whole[:LAYER])
        copies.append(pltpu.make_async_copy(fields.at[field], out_ref.at[0, field], semaphores.at[field]))
        copies[-1].start()
    for copy in copies:
        copy.wait()


SHIFTS_A = (0, 1, -1, 2, -2)
SHIFTS_B = (0, 1, -1)
FAR_A = (3, -3)
FAR_B = (2, -2)
NEAR = len(SHIFTS_A) + len(SHIFTS_B)
BLOCKS = NEAR + len(FAR_A) + len(FAR_B)
RING = 8
ENTRIES = 256 + FIELDS * 128
PACKED = ((0, 64, 64), (64, 64, 96), (128, 8, 8), (136, 8, 24), (144, FIELDS, FIELDS), (152, 8, 64), (160, 64, 8))


def face_weights(shape, per_edge, node, weights):
    column = iota(shape, 1)
    face = column // (per_edge * per_edge)
    trace = column % (per_edge * per_edge)
    a, b, c = (node // (per_edge * per_edge), (node // per_edge) % per_edge, node % per_edge)
    first = [a, a, b, b, c, c]
    rest = [b * per_edge + c] * 2 + [a * per_edge + c] * 2 + [a * per_edge + b] * 2
    result = jnp.zeros(shape, F32)
    for which, weight in weights.items():
        edge = per_edge - 1 if which % 2 == 0 else 0
        on = (face == which) & (first[which] == edge) & (rest[which] == trace)
        result = jnp.where(on, weight, result)
    return result


def split(value):
    high = value.astype(BF16)
    return high, (value - high.astype(F32)).astype(BF16)


def bdot(a, b):
    return jnp.dot(a, b, preferred_element_type=F32)


def operators_kernel(
    packed_ref,
    level_ref,
    chain_high_ref,
    chain_low_ref,
    prolong_high_ref,
    prolong_low_ref,
    near_high_ref,
    near_low_ref,
    far_ref,
):
    volume, lift, coarse_volume, clift, mixing, restriction, prolongation = (
        packed_ref[first : first + rows, :columns] for first, rows, columns in PACKED
    )
    fine_ref = level_ref.at[:256]
    restrict_all_ref = level_ref.at[256:ENTRIES]
    place = lax.axis_index("space")
    kx, ky, kx_other, ky_other, paired = wave_numbers(place & (UNITS - 1))
    single = paired == 0

    def turn_cos(first, second, second_half):
        return jnp.where(second_half, eighth_cos(second), eighth_cos(first))

    def put_packed(ref, rows, value):
        high, low = split(value)
        ref[rows, :128] = high
        ref[rows, 128:] = low

    def put(high_ref, low_ref, rows, columns, value):
        high, low = split(value)
        high_ref[rows, columns] = high
        low_ref[rows, columns] = low

    wide = iota((128, 128), 1)
    tall = iota((128, 128), 0)
    row = iota((128, 96), 0)
    half = row >= 64
    same = (wide >= 64) == (tall >= 64)
    cos_x = turn_cos(kx, kx_other, half)
    cos_y = turn_cos(ky, ky_other, half)
    sin_x = jnp.where(single, 0.0, eighth_cos(kx - 2))
    sin_y = jnp.where(single, 0.0, eighth_cos(ky - 2))
    sign = jnp.where(half, -1.0, 1.0)
    along = face_weights((128, 96), 4, row & 63, {0: cos_x, 1: cos_x, 2: cos_y, 3: cos_y})
    across = face_weights(
        (128, 96), 4, row & 63, {0: -sin_x * sign, 1: sin_x * sign, 2: -sin_y * sign, 3: sin_y * sign}
    )
    ahead = face_weights((128, 96), 4, row & 63, {4: 1.0, 5: 1.0})
    lift2 = jnp.concatenate([lift] * 2, axis=0)
    volume2 = jnp.concatenate([volume] * 2, axis=0)
    twice = jnp.where((iota((128, 64), 0) & 63) == iota((128, 64), 1), 1.0, 0.0).astype(F32)
    inside = (DT / 2) * jnp.where(same, nt(twice, volume2) + nt(along, lift2), nt(across, lift2))
    beside = (DT / 2) * jnp.where(same, nt(ahead, lift2), 0.0)
    put_packed(fine_ref, slice(0, 128), inside)
    put_packed(fine_ref, slice(128, 256), beside)
    psi = jnp.concatenate([inside, beside], axis=0)

    row = iota((128, 24), 0)
    half = ((row >> 3) & 1) == 1
    cos_x = turn_cos(kx, kx_other, half)
    cos_y = turn_cos(ky, ky_other, half)
    sign = jnp.where(half, -1.0, 1.0)
    along = face_weights((128, 24), 2, row & 7, {0: cos_x, 1: cos_x, 2: cos_y, 3: cos_y})
    across = face_weights(
        (128, 24), 2, row & 7, {0: -sin_x * sign, 1: sin_x * sign, 2: -sin_y * sign, 3: sin_y * sign}
    )
    ahead = face_weights((128, 24), 2, row & 7, {4: 1.0, 5: 1.0})
    node8 = jnp.where((iota((128, 8), 0) & 7) == iota((128, 8), 1), 1.0, 0.0).astype(F32)
    field8 = jnp.where((iota((128, FIELDS), 0) >> 4) == iota((128, FIELDS), 1), 1.0, 0.0).astype(F32)
    same = ((wide >> 3) & 1) == ((tall >> 3) & 1)
    number = iota((32, FIELDS), 0)
    entries = nn(jnp.where(number // FIELDS == iota((32, FIELDS), 1), 1.0, 0.0).astype(F32), mixing)
    entries = jnp.where(number % FIELDS == iota((32, FIELDS), 1), entries, 0.0)
    entries = jnp.broadcast_to(jnp.sum(entries, axis=1, keepdims=True), (32, 128))
    high, middle = split(entries)
    low = (entries - high.astype(F32) - middle.astype(F32)).astype(BF16)
    level_ref[ENTRIES : ENTRIES + 32, :128] = high
    level_ref[ENTRIES : ENTRIES + 32, 128:] = middle
    level_ref[ENTRIES + 32 :, :128] = low
    level_ref[ENTRIES + 32 :, 128:] = jnp.zeros((32, 128), BF16)
    power = nt(field8, mixing)
    coupled = [nt(field8, field8), nt(power, field8)]
    for _ in range(2):
        power = nt(power, mixing)
        coupled.append(nt(power, field8))
    along = nt(nt(node8, coarse_volume) + nt(along, clift), node8)
    across = nt(nt(across, clift), node8)
    ahead = nt(nt(ahead, clift), node8)
    level = DT * coupled[1] * jnp.where(same, along, across)
    beside = DT * coupled[1] * jnp.where(same, ahead, 0.0)
    upper = (tall & 1) == 1
    below = jnp.where(upper, beside, 0.0)
    above = jnp.where(upper, 0.0, beside)
    level_level = nn(level, level)
    below_all = nn(below, jnp.concatenate([level, below, above], axis=1))
    above_all = nn(above, jnp.concatenate([level, below, above], axis=1))
    once = [level, below, above, jnp.zeros((128, 128), F32)]
    squared = [
        level_level + below_all[:, 256:] + above_all[:, 128:256],
        nn(level, below) + below_all[:, :128],
        nn(level, above) + above_all[:, :128],
        below_all[:, 128:256] + above_all[:, 256:],
    ]
    for block in range(4):
        rows = slice(block * 128, (block + 1) * 128)
        put(chain_high_ref, chain_low_ref, rows, slice(0, 128), once[block])
        put(chain_high_ref, chain_low_ref, rows, slice(128, 256), 0.5 * squared[block])

    restricting = nt(twice, nn(node8, restriction))
    prolonging = nt(node8, jnp.concatenate([prolongation] * 2, axis=0))
    down = (tall >= 64) == (((wide >> 3) & 1) == 1)
    up = (wide >= 64) == (((tall >> 3) & 1) == 1)
    restricting = jnp.where(down, restricting, 0.0)
    prolonging = jnp.where(up, prolonging, 0.0)
    for field in range(FIELDS):
        part = slice(field * 128, (field + 1) * 128)
        put_packed(restrict_all_ref, part, jnp.where((wide >> 4) == field, restricting, 0.0))
        value = jnp.where((tall >> 4) == field, prolonging, 0.0)
        put(prolong_high_ref, prolong_low_ref, slice(0, 128), part, value)
        prolong_high_ref[128:, part] = value.astype(BF16)

    response = jnp.where(tall < 16, prolonging, 0.0)
    fine_below = (wide & 3) == 3
    responses = [nn(response, restricting)]
    for _ in range(3):
        near = jnp.where(fine_below, pltpu.roll(response, 16, 0), pltpu.roll(response, 112, 0))
        response = nn(jnp.concatenate([response, near], axis=1), psi)
        responses.append(nn(response, restricting))

    def block(shift, weights):
        rows = slice((shift % RING) * 16, (shift % RING) * 16 + 16)
        total = jnp.zeros((128, 128), F32)
        for order, weight in weights.items():
            if abs(shift) <= order:
                total = total + weight * coupled[order] * jnp.concatenate([responses[order][rows]] * 8, axis=0)
        return total

    kinds = [(shift, 0) for shift in SHIFTS_A] + [(shift, 1) for shift in SHIFTS_B]
    kinds += [(shift, 0) for shift in FAR_A] + [(shift, 1) for shift in FAR_B]
    ends = ({0: 1.0, 1: 2.0, 2: 1.0}, {0: 2.0, 1: 1.0})
    mid_rates = ({1: 1.0, 2: 1.0}, {1: 1.0})
    end_rates = ({1: 1.0, 2: 2.0, 3: 1.0}, {1: 2.0, 2: 1.0})
    for index, (shift, kind) in enumerate(kinds):
        rows = slice(index * 128, (index + 1) * 128)
        if index < NEAR:
            put(near_high_ref, near_low_ref, rows, slice(0, 128), block(shift, ends[kind]))
            put(near_high_ref, near_low_ref, rows, slice(128, 256), block(shift, mid_rates[kind]))
        put_packed(far_ref, rows, block(shift, end_rates[kind]))


def shifted(even, odd, shift):
    def rolled(value, by):
        return value if by == 0 else pltpu.roll(value, by % len(value), 0)

    if shift % 2 == 0:
        return rolled(even, shift // 2), rolled(odd, shift // 2)
    return rolled(odd, (shift + 1) // 2), rolled(even, (shift - 1) // 2)


def beside_layers(state, from_below, reach=1):
    half = len(state) // 2
    even, odd = state[:half], state[half:]
    below = shifted(even, odd, reach)
    above = shifted(even, odd, -reach)
    return jnp.concatenate([jnp.where(from_below, low, high) for low, high in zip(below, above)], axis=0)


def moved(state, shift):
    return jnp.concatenate(shifted(state[:LAYER], state[LAYER:], shift), axis=0)


def polynomials():
    once = np.array([1.0, 1.0])
    twice = np.polymul(once, once)
    two = np.array([1.0, 2.0])
    on_start = np.array([5 / 12, 4 / 3, 1.0])
    on_mid = np.array([2 / 3, 1 / 3, 0.0])
    on_end = np.array([-1 / 12, 1 / 3, 0.0])
    own = np.polyadd(np.polymul(on_mid, once), np.polymul(on_end, twice))
    table = {
        "first": np.polyadd(on_start, own),
        "later": np.polyadd(np.polymul(on_start, twice), own),
        "head": own,
        "push": np.polyadd(on_mid, np.polymul(on_end, two)),
        "head_before": np.polymul(on_start, twice),
        "push_before": np.polymul(on_start, two),
        "new_head": twice,
        "new_push": two,
    }
    return {name: [float(x) for x in np.pad(p[::-1], (0, 5 - len(p)))] for name, p in table.items()}


def iterate_kernel(
    slices,
    received_ref,
    level_ref,
    chain_high_ref,
    chain_low_ref,
    prolong_high_ref,
    prolong_low_ref,
    near_high_ref,
    near_low_ref,
    far_ref,
    sent_ref,
    mixing_ref,
    start,
    head1,
    rate1,
    head2,
    rate2,
    ends,
    ends_rate,
):
    fine_ref = level_ref.at[:256]
    restrict_all_ref = level_ref.at[256:ENTRIES]
    mixing_ref[...] = (
        level_ref[ENTRIES : ENTRIES + 32, :128].astype(F32)
        + level_ref[ENTRIES : ENTRIES + 32, 128:].astype(F32)
        + level_ref[ENTRIES + 32 :, :128].astype(F32)
    )
    place = lax.axis_index("space")
    mine = lax.axis_index("tm")
    kx, ky, kx_other, ky_other, paired = wave_numbers(place & (UNITS - 1))
    single = paired == 0
    lane = iota((LAYER, 128), 1)
    fine_below = (lane & 3) == 3
    coarse_below = (lane & 1) == 1
    halved = lane >= 64

    def packed_dot(value, packed):
        high, low = split(value)
        both = bdot(high, packed)
        return both[:, :128] + (both[:, 128:] + bdot(low, packed[:, :128]))

    def dot3(value, high_op, low_op):
        high, low = split(value)
        return bdot(high, high_op) + (bdot(high, low_op) + bdot(low, high_op))

    def fields_of(state):
        rows = len(state) // FIELDS
        return [state[field * rows : (field + 1) * rows] for field in range(FIELDS)]

    def psi(state):
        parts = fields_of(state)
        pieces = []
        for field in range(FIELDS):
            first = field * FIELDS
            mixed = mixing_ref[first : first + 1] * parts[0]
            for other in range(1, FIELDS):
                mixed = mixed + mixing_ref[first + other : first + other + 1] * parts[other]
            pieces.append(jnp.concatenate([mixed, beside_layers(mixed, fine_below[: len(mixed) // 2])], axis=1))
        return packed_dot(jnp.concatenate(pieces, axis=0), fine_ref[...])

    def restrict(state):
        return packed_dot(jnp.concatenate(fields_of(state), axis=1), restrict_all_ref[...])

    def stages(states):
        wide = [
            jnp.concatenate(
                [state, moved(state, 1), moved(state, -1), beside_layers(state, coarse_below, 2)], axis=1
            )
            for state in states
        ]
        both = dot3(jnp.concatenate(wide, axis=0), chain_high_ref[...], chain_low_ref[...])
        both = [both[i * 128 : (i + 1) * 128] for i in range(len(states))]
        return [(part[:, :128], part[:, 128:]) for part in both]

    def in_order(column):
        begin = column if column < STATE else 2 * STATE
        own = received_ref[:, 0, begin : begin + 128]
        if column < STATE:
            other = received_ref[:, 0, STATE + column : STATE + column + 128]
        else:
            other = pltpu.roll(own, 124, 1)
        return jnp.concatenate([other[:EDGE], own, other[EDGE:]], axis=0)

    shifts = in_order(STATE)
    lower_triangle = jnp.where(iota((LAYER, LAYER), 1) < iota((LAYER, LAYER), 0), 1.0, 0.0).astype(F32)
    first_x, first_y = shifts[:, 0:1], shifts[:, 1:2]
    both_x, both_y = first_x + shifts[:, 2:3], first_y + shifts[:, 3:4]
    passed_x = nn(lower_triangle, jnp.broadcast_to(both_x, (LAYER, 128)))
    passed_y = nn(lower_triangle, jnp.broadcast_to(both_y, (LAYER, 128)))
    turning = []
    for add_x, add_y in ((first_x, first_y), (both_x, both_y)):
        shift_x = (passed_x + add_x).astype(jnp.int32)
        shift_y = (passed_y + add_y).astype(jnp.int32)
        turns = jnp.where(halved, kx_other, kx) * shift_x + jnp.where(halved, ky_other, ky) * shift_y
        cos = eighth_cos(turns)
        sin = jnp.where(single, 0.0, eighth_cos(turns - 2))
        turning.append((cos, jnp.where(halved, sin, -sin)))

    for field in range(FIELDS):
        for index in range(2):
            value = in_order((field * 2 + index) * 128)
            cos, sin = turning[index]
            begin = field * 128 + index * LAYER
            start[begin : begin + LAYER] = value * cos + pltpu.roll(value, 64, 1) * sin

    initial = start[...]
    power = psi(initial)
    begin = restrict(initial)
    power_coarse = [begin, restrict(power)]
    ((begin_rate, begin_twice),) = stages([begin])
    defect = 2.0 * power_coarse[1] - begin_rate
    head, rate = begin, begin_rate
    later_head, later_rate = begin, begin_rate
    old_rate, old_twice, last = begin_rate, begin_twice, power_coarse[1]
    head1[0], rate1[0] = begin, begin_rate
    head2[0], rate2[0] = begin, begin_rate
    ends[0], ends_rate[0] = begin, begin_rate

    def needed(change, push):
        kinds = [(shift, change) for shift in SHIFTS_A] + [(shift, push) for shift in SHIFTS_B]
        kinds += [(shift, change) for shift in FAR_A] + [(shift, push) for shift in FAR_B]
        parts = [split(moved(value, shift)) for shift, value in kinds]
        high = jnp.concatenate([part[0] for part in parts], axis=1)
        low = jnp.concatenate([part[1] for part in parts], axis=1)
        near_high, near_low = high[:, : NEAR * 128], low[:, : NEAR * 128]
        near = bdot(near_high, near_high_ref[...]) + (
            bdot(near_high, near_low_ref[...]) + bdot(near_low, near_high_ref[...])
        )
        far = bdot(high, far_ref[...])
        return near[:, :128], near[:, 128:], far[:, :128] + (far[:, 128:] + bdot(low, far_ref[:, :128]))

    previous = jnp.maximum(mine - 1, 0)
    later = jnp.where(mine > 0, 1.0, 0.0).astype(F32)
    table = polynomials()

    def around(state):
        half = len(state) // 2
        return jnp.concatenate(
            [state[EDGE - MARGIN : EDGE + UNITS + MARGIN], state[half + EDGE - MARGIN : half + EDGE + UNITS + MARGIN]],
            axis=0,
        )

    initial_around = jnp.concatenate([around(part) for part in fields_of(initial)], axis=0)

    def added(order):
        total = None
        for name, value in parts.items():
            if table[name][order] != 0.0:
                term = table[name][order] * value
                total = term if total is None else total + term
        high, low = split(total)
        wide = bdot(jnp.concatenate([high, low], axis=1), prolong_high_ref[...])
        wide = wide + bdot(high, prolong_low_ref[...])
        wide = jnp.concatenate([wide[:, f * 128 : (f + 1) * 128] for f in range(FIELDS)], axis=0)
        weight = jnp.where(mine > 0, table["later"][order], table["first"][order]).astype(F32)
        return wide + weight * initial_around

    waiting = []
    ready = None
    for step in range(slices + 2):
        states = []
        if step < slices:
            states.append(rate + defect)
        if ready is not None:
            tail = ready[0] + end_start
            next_last = ready[2] + end_rate_start
            integral = (last + 4.0 * (ready[1] + mid_rate_start) + next_last) * (1.0 / 3.0)
            later_defect = integral - old_rate
            states += [tail, later_rate + later_defect]
        found = stages(states)
        if ready is not None:
            (tail_rate, tail_twice), (once, half_twice) = found[-2:]
            later_head = later_head + later_rate + later_defect + 0.5 * (old_rate - tail_rate + once)
            later_rate = later_rate + once + half_twice + (old_twice - tail_twice)
            old_rate, old_twice, last = tail_rate, tail_twice, next_last
            slot = step - 1
            head2[slot], rate2[slot] = later_head, later_rate
            ends[slot], ends_rate[slot] = tail, tail_rate
        ready = needed(*waiting.pop()) if waiting else None
        if step < slices:
            once, half_twice = found[0]
            change = head - begin
            head, next_rate = head + rate + defect + 0.5 * once, rate + once + half_twice
            waiting.append((change, (next_rate - rate) * 0.125))
            rate = next_rate
            head1[step + 1], rate1[step + 1] = head, rate
        if step == slices - 1:
            parts = {
                "head": around(head1[mine] - begin),
                "push": around((rate1[mine + 1] - rate1[mine]) * 0.125),
                "head_before": around((head1[previous] - begin) * later),
                "push_before": around((rate1[mine] - rate1[previous]) * (0.125 * later)),
            }
            state = added(4)
            state = psi(state) + added(3)
        if step < 2:
            power = psi(power)
            power_coarse.append(restrict(power))
        if step == 1:
            end_start = power_coarse[0] + 2.0 * power_coarse[1] + power_coarse[2]
            mid_rate_start = power_coarse[1] + power_coarse[2]
            end_rate_start = power_coarse[1] + 2.0 * power_coarse[2] + power_coarse[3]

    new_head = head2[mine] - ends[mine]
    new_push = ((rate2[mine + 1] - ends_rate[mine + 1]) - (rate2[mine] - ends_rate[mine])) * 0.125
    parts["new_head"], parts["new_push"] = around(new_head), around(new_push)
    for order in (2, 1, 0):
        state = psi(state) + added(order)
    turned = [(cos[EDGE - MARGIN : EDGE + UNITS + MARGIN], sin[EDGE - MARGIN : EDGE + UNITS + MARGIN]) for cos, sin in turning]
    rows = len(state) // (2 * FIELDS)
    for field in range(FIELDS):
        for index in range(2):
            cos, sin = turned[index]
            begin_row = (field * 2 + index) * rows
            value = state[begin_row : begin_row + rows]
            value = value * cos - pltpu.roll(value, 64, 1) * sin
            column = (field * 2 + index) * 128
            sent_ref[:, 0, column : column + 128] = value[MARGIN : MARGIN + UNITS]


IN_VMEM = pl.BlockSpec(memory_space=pltpu.VMEM)


def operators_call(volume_op, lift_op, coarse_volume, coarse_lift, mixing, restrict_op, prolong_op):
    shapes = [
        (ENTRIES + 64, 256),
        (512, 256),
        (512, 256),
        (256, FIELDS * 128),
        (128, FIELDS * 128),
        (NEAR * 128, 256),
        (NEAR * 128, 256),
        (BLOCKS * 128, 256),
    ]
    operands = (volume_op, lift_op, coarse_volume, coarse_lift, mixing, restrict_op, prolong_op)
    packed = jnp.zeros((224, 128), F32)
    for operand, (first, rows, columns) in zip(operands, PACKED):
        packed = packed + jnp.pad(operand, ((first, 224 - first - rows), (0, 128 - columns)))
    return pl.pallas_call(
        operators_kernel,
        out_shape=[jax.ShapeDtypeStruct(shape, BF16) for shape in shapes],
        in_specs=[IN_VMEM],
        out_specs=[IN_VMEM] * len(shapes),
        compiler_params=pltpu.CompilerParams(vmem_limit_bytes=VMEM_LIMIT),
        cost_estimate=pl.CostEstimate(flops=10**8, bytes_accessed=3 * 10**6, transcendentals=0),
        name="operators",
    )(packed)


def iterate_kernel_call(slices, received, operators):
    coarse_shape = pltpu.VMEM((slices + 1, 128, 128), F32)
    return pl.pallas_call(
        functools.partial(iterate_kernel, slices),
        out_shape=jax.ShapeDtypeStruct((UNITS, 1, STATE), F32),
        in_specs=[IN_VMEM] * (1 + len(operators)),
        out_specs=IN_VMEM,
        scratch_shapes=[pltpu.VMEM((32, 128), F32), pltpu.VMEM((FIELDS * 128, 128), F32)]
        + [coarse_shape] * 6,
        compiler_params=pltpu.CompilerParams(vmem_limit_bytes=VMEM_LIMIT),
        name="iterate",
    )(received, *operators)


def iterate_call(slices, received, volume_op, lift_op, coarse_volume, coarse_lift, mixing, restrict_op, prolong_op):
    operators = operators_call(
        volume_op, lift_op, coarse_volume, coarse_lift, mixing, restrict_op, prolong_op
    )
    return iterate_kernel_call(slices, received[:, None, :], operators)


def window_partners(slices, places):
    per_chip_row = 8
    depth = places // per_chip_row
    ring = 2 * depth
    route = []
    for slot in range(slices):
        for place in range(places):
            z = slot % 2 * depth + place // per_chip_row
            other = (z - 2 if z % 4 < 2 else z + 2) % ring
            partner = (slot - slot % 2 + other // depth) * places + other % depth * per_chip_row
            route.append((partner + place % per_chip_row, slot * places + place))
    return route


def on_device(
    initial,
    neighbours,
    volume_op,
    lift_op,
    coarse_volume,
    coarse_lift,
    mixing,
    restrict_op,
    prolong_op,
):
    params = pltpu.CompilerParams(vmem_limit_bytes=VMEM_LIMIT)
    route = window_partners(lax.axis_size("tm"), lax.axis_size("space"))
    state = initial.reshape(FIELDS * LAYER, -1)
    state_beside = lax.ppermute(state, ("tm", "space"), route)
    links_beside = lax.ppermute(neighbours, ("tm", "space"), route)
    modes, basis = pl.pallas_call(
        own_modes_kernel,
        out_shape=(
            jax.ShapeDtypeStruct((UNITS, STATE + 128), F32),
            jax.ShapeDtypeStruct((LAYER, 128), F32),
        ),
        in_specs=[IN_VMEM] * 2,
        out_specs=(IN_VMEM, IN_VMEM),
        compiler_params=params,
        name="own_modes",
    )(state, neighbours)
    sent = pl.pallas_call(
        both_modes_kernel,
        out_shape=jax.ShapeDtypeStruct((UNITS, 1, 2 * STATE + 128), F32),
        in_specs=[IN_VMEM] * 3,
        out_specs=pl.BlockSpec(memory_space=pl.ANY),
        scratch_shapes=[
            pltpu.VMEM((UNITS, 1, 2 * STATE + 128), F32),
            pltpu.SemaphoreType.DMA((2,)),
        ],
        compiler_params=params,
        name="both_modes",
    )(modes, state_beside, links_beside)
    windows = [[first + i for i in range(UNITS)] for first in range(0, lax.axis_size("space"), UNITS)]

    def exchange(blocks):
        return lax.all_to_all(blocks, "space", 0, 0, axis_index_groups=windows, tiled=True)

    received = exchange(sent)
    operators = operators_call(
        volume_op, lift_op, coarse_volume, coarse_lift, mixing, restrict_op, prolong_op
    )
    modes = iterate_kernel_call(lax.axis_size("tm"), received, operators)
    returned = exchange(modes)
    return pl.pallas_call(
        from_modes_kernel,
        out_shape=jax.ShapeDtypeStruct((1, FIELDS, LAYER, 128), F32),
        in_specs=[IN_VMEM] * 2,
        out_specs=pl.BlockSpec(memory_space=pl.ANY),
        scratch_shapes=[pltpu.VMEM((FIELDS, LAYER, 128), F32), pltpu.SemaphoreType.DMA((FIELDS,))],
        compiler_params=params,
        name="from_modes",
    )(returned, basis)


def solution(mesh):
    return jax.shard_map(
        on_device,
        mesh=mesh,
        in_specs=(P(None, None, "space"), P(None, "space"), P(), P(), P(), P(), P(), P(), P()),
        out_specs=P("tm", None, None, "space"),
        check_vma=False,
    )
```

```python
import functools

import jax
import jax.numpy as jnp
import numpy as np
from jax import lax
from jax.experimental import pallas as pl
from jax.experimental.pallas import tpu as pltpu
from jax.sharding import PartitionSpec as P

LAYER = 64
FIELDS = 5
DT = 0.125
HALF = 0.7071067811865476
UNITS = 32
STATE = FIELDS * 2 * 128
EDGE = 16
MARGIN = 8
EXACT = lax.Precision.HIGHEST
F32 = jnp.float32
BF16 = jnp.bfloat16
VMEM_LIMIT = 20 * 1024 * 1024


def iota(shape, dim):
    return lax.broadcasted_iota(jnp.int32, shape, dim)


def nn(a, b):
    return lax.dot_general(a, b, (((1,), (0,)), ((), ())), precision=EXACT, preferred_element_type=F32)


def nt(a, b):
    return lax.dot_general(a, b, (((1,), (1,)), ((), ())), precision=EXACT, preferred_element_type=F32)


def nt3(a, b):
    dims = (((1,), (1,)), ((), ()))
    return lax.dot_general(a, b, dims, precision=lax.Precision.HIGH, preferred_element_type=F32)


def eighth_cos(turn):
    turn = turn & 7
    diagonal = jnp.where((turn == 1) | (turn == 7), HALF, jnp.where((turn == 3) | (turn == 5), -HALF, 0.0))
    return jnp.where(turn == 0, 1.0, jnp.where(turn == 4, -1.0, diagonal)).astype(F32)


def wave_numbers(unit):
    low = unit - 23
    high = unit - 26
    kx = jnp.where(unit < 24, unit & 7, jnp.where(unit < 27, low, jnp.where(unit < 30, high, 0)))
    ky = jnp.where(unit < 24, 1 + (unit >> 3), jnp.where(unit < 27, 0, jnp.where(unit == 30, 0, 4)))
    paired = jnp.where(unit < 30, 1, 0)
    kx_other = jnp.where(unit < 30, kx, 4)
    return kx, ky, kx_other, ky, paired


def grid_places(links, base, total, first_slot):
    lane = iota((1, 128), 1)
    upper = lane >= LAYER
    target = iota((128, 128), 0)

    def steps(face):
        one = jnp.where(links[face : face + 1] - base == target, 1.0, 0.0).astype(BF16)
        two = jnp.dot(one, one, preferred_element_type=F32).astype(BF16)
        four = jnp.dot(two, two, preferred_element_type=F32).astype(BF16)
        return one, two, four

    row = iota((8, 128), 0)
    found = jnp.where((row == 0) & ((iota((8, 128), 1) & (LAYER - 1)) == 0), 1.0, 0.0).astype(F32)
    for part, moves in ((1, steps(0)), (2, steps(2))):
        for power, move in enumerate(moves):
            shifted = jnp.dot(found.astype(BF16), move, preferred_element_type=F32)
            found = found + shifted + jnp.where(row == part, shifted[0:1] * (1 << power), 0.0)
    along_x = found[1:2]
    along_y = found[2:3]

    below = jnp.where(upper, base, (base + total - LAYER) % total)
    hit = links[4:5] == below
    extra = jnp.zeros((1, 128), F32)
    for slot, (layer_upper, value) in enumerate(
        ((False, along_x), (False, along_y), (True, along_x), (True, along_y))
    ):
        part = jnp.where(hit & (upper == layer_upper), value, 0.0)
        extra = jnp.where(lane == first_slot + slot, jnp.sum(part, axis=1, keepdims=True), extra)
    return along_x.astype(jnp.int32), along_y.astype(jnp.int32), extra


def layer_modes(ref, links, where, places, first_slot):
    upper = iota((1, 128), 1) >= LAYER
    halved = iota((UNITS, 128), 1) >= LAYER
    mode = iota((LAYER, 128), 0)
    kx, ky, kx_other, ky_other, paired = wave_numbers(mode & (UNITS - 1))
    second = mode >= UNITS
    along_x, along_y, extra = grid_places(links, where * 2 * LAYER, places * 2 * LAYER, first_slot)
    turns = jnp.where(second, kx_other, kx) * along_x + jnp.where(second, ky_other, ky) * along_y
    basis = eighth_cos(turns + jnp.where(second, 2 * paired, 0))
    apart = jnp.concatenate([jnp.where(upper, 0.0, basis), jnp.where(upper, basis, 0.0)], axis=0)

    def of_field(field):
        state = ref[field * LAYER : (field + 1) * LAYER]
        modes = nt3(apart, jnp.concatenate([state, state], axis=0))
        return [
            jnp.where(
                halved,
                modes[index * LAYER + UNITS : (index + 1) * LAYER],
                modes[index * LAYER : index * LAYER + UNITS],
            )
            for index in range(2)
        ]

    return basis, of_field, extra


def own_modes_kernel(own_ref, links_ref, sent_ref, basis_ref, blocks, semaphore):
    basis, modes_of, extra = layer_modes(own_ref, links_ref[...], lax.axis_index("space"), lax.axis_size("space"), 0)
    for field in range(FIELDS):
        for index, value in enumerate(modes_of(field)):
            column = (field * 2 + index) * 128
            blocks[:, 0, column : column + 128] = value
    copy = pltpu.make_async_copy(blocks, sent_ref.at[:, :, :STATE], semaphore)
    copy.start()
    basis_ref[:LAYER] = basis
    basis_ref[LAYER:] = jnp.broadcast_to(extra, (8, 128))
    copy.wait()


def beside_modes_kernel(half_ref, basis_ref, beside_ref, links_ref, sent_ref, blocks, semaphores):
    del half_ref
    place = lax.axis_index("space")
    places = lax.axis_size("space")
    partner = (jnp.where(((place >> 3) & 3) < 2, place - EDGE, place + EDGE) + places) % places
    copies = []

    def send(first, columns):
        part = pltpu.make_async_copy(
            blocks.at[:, :, first : first + columns],
            sent_ref.at[:, :, STATE + first : STATE + first + columns],
            semaphores.at[len(copies)],
        )
        part.start()
        copies.append(part)

    _, modes_of, extra = layer_modes(beside_ref, links_ref[...], partner, places, 4)
    for field in range(FIELDS):
        for index, value in enumerate(modes_of(field)):
            column = (field * 2 + index) * 128
            blocks[:, 0, column : column + 128] = value
        send(field * 256, 256)
    blocks[:, 0, STATE:] = jnp.broadcast_to(basis_ref[LAYER : LAYER + 1] + extra, (UNITS, 128))
    send(STATE, 128)
    for copy in copies:
        copy.wait()


def from_modes_kernel(modes_ref, basis_ref, out_ref, fields, semaphores):
    copies = []
    unit = iota((LAYER, 128), 0) & (UNITS - 1)
    scale = jnp.where(unit < 30, 2.0 / LAYER, 1.0 / LAYER).astype(F32)
    back = basis_ref[:LAYER] * scale
    upper = iota((LAYER, 128), 1) >= LAYER
    halved = iota((UNITS, 128), 1) >= LAYER
    for field in range(FIELDS):
        column = field * 256
        even = modes_ref[:, 0, column : column + 128]
        odd = modes_ref[:, 0, column + 128 : column + 256]
        real = jnp.where(halved, pltpu.roll(odd, 64, 1), even)
        imaginary = jnp.where(halved, odd, pltpu.roll(even, 64, 1))
        whole = nn(jnp.transpose(jnp.concatenate([real, imaginary], axis=0)), back)
        fields[field] = jnp.where(upper, whole[LAYER:], whole[:LAYER])
        copies.append(pltpu.make_async_copy(fields.at[field], out_ref.at[0, field], semaphores.at[field]))
        copies[-1].start()
    for copy in copies:
        copy.wait()


SHIFTS_A = (0, 1, -1, 2, -2)
SHIFTS_B = (0, 1, -1)
FAR_A = (3, -3)
FAR_B = (2, -2)
NEAR = len(SHIFTS_A) + len(SHIFTS_B)
BLOCKS = NEAR + len(FAR_A) + len(FAR_B)
RING = 8
RESTRICT = 256
PROLONG = RESTRICT + FIELDS * 128
ENTRIES = PROLONG + 128
PACKED = ((0, 64, 64), (64, 64, 96), (128, 8, 8), (136, 8, 24), (144, FIELDS, FIELDS), (152, 8, 64), (160, 64, 8))


def face_weights(shape, per_edge, node, weights):
    column = iota(shape, 1)
    face = column // (per_edge * per_edge)
    trace = column % (per_edge * per_edge)
    a, b, c = (node // (per_edge * per_edge), (node // per_edge) % per_edge, node % per_edge)
    first = [a, a, b, b, c, c]
    rest = [b * per_edge + c] * 2 + [a * per_edge + c] * 2 + [a * per_edge + b] * 2
    result = jnp.zeros(shape, F32)
    for which, weight in weights.items():
        edge = per_edge - 1 if which % 2 == 0 else 0
        on = (face == which) & (first[which] == edge) & (rest[which] == trace)
        result = jnp.where(on, weight, result)
    return result


def split(value):
    high = value.astype(BF16)
    return high, (value - high.astype(F32)).astype(BF16)


def bdot(a, b):
    return jnp.dot(a, b, preferred_element_type=F32)


def operators_kernel(
    packed_ref,
    level_ref,
    chain_high_ref,
    chain_low_ref,
    near_high_ref,
    near_low_ref,
    far_ref,
):
    volume, lift, coarse_volume, clift, mixing, restriction, prolongation = (
        packed_ref[first : first + rows, :columns] for first, rows, columns in PACKED
    )
    fine_ref = level_ref.at[:256]
    place = lax.axis_index("space")
    kx, ky, kx_other, ky_other, paired = wave_numbers(place & (UNITS - 1))
    single = paired == 0

    def turn_cos(first, second, second_half):
        return jnp.where(second_half, eighth_cos(second), eighth_cos(first))

    def put_packed(ref, rows, value):
        high, low = split(value)
        ref[rows, :128] = high
        ref[rows, 128:] = low

    def put(high_ref, low_ref, rows, columns, value):
        high, low = split(value)
        high_ref[rows, columns] = high
        low_ref[rows, columns] = low

    wide = iota((128, 128), 1)
    tall = iota((128, 128), 0)
    row = iota((128, 96), 0)
    half = row >= 64
    same = (wide >= 64) == (tall >= 64)
    cos_x = turn_cos(kx, kx_other, half)
    cos_y = turn_cos(ky, ky_other, half)
    sin_x = jnp.where(single, 0.0, eighth_cos(kx - 2))
    sin_y = jnp.where(single, 0.0, eighth_cos(ky - 2))
    sign = jnp.where(half, -1.0, 1.0)
    along = face_weights((128, 96), 4, row & 63, {0: cos_x, 1: cos_x, 2: cos_y, 3: cos_y})
    across = face_weights(
        (128, 96), 4, row & 63, {0: -sin_x * sign, 1: sin_x * sign, 2: -sin_y * sign, 3: sin_y * sign}
    )
    ahead = face_weights((128, 96), 4, row & 63, {4: 1.0, 5: 1.0})
    lift2 = jnp.concatenate([lift] * 2, axis=0)
    volume2 = jnp.concatenate([volume] * 2, axis=0)
    twice = jnp.where((iota((128, 64), 0) & 63) == iota((128, 64), 1), 1.0, 0.0).astype(F32)
    inside = (DT / 2) * jnp.where(same, nt(twice, volume2) + nt(along, lift2), nt(across, lift2))
    beside = (DT / 2) * jnp.where(same, nt(ahead, lift2), 0.0)
    put_packed(fine_ref, slice(0, 128), inside)
    put_packed(fine_ref, slice(128, 256), beside)
    psi = jnp.concatenate([inside, beside], axis=0)

    row = iota((128, 24), 0)
    half = ((row >> 3) & 1) == 1
    cos_x = turn_cos(kx, kx_other, half)
    cos_y = turn_cos(ky, ky_other, half)
    sign = jnp.where(half, -1.0, 1.0)
    along = face_weights((128, 24), 2, row & 7, {0: cos_x, 1: cos_x, 2: cos_y, 3: cos_y})
    across = face_weights(
        (128, 24), 2, row & 7, {0: -sin_x * sign, 1: sin_x * sign, 2: -sin_y * sign, 3: sin_y * sign}
    )
    ahead = face_weights((128, 24), 2, row & 7, {4: 1.0, 5: 1.0})
    node8 = jnp.where((iota((128, 8), 0) & 7) == iota((128, 8), 1), 1.0, 0.0).astype(F32)
    field8 = jnp.where((iota((128, FIELDS), 0) >> 4) == iota((128, FIELDS), 1), 1.0, 0.0).astype(F32)
    same = ((wide >> 3) & 1) == ((tall >> 3) & 1)
    number = iota((32, FIELDS), 0)
    entries = nn(jnp.where(number // FIELDS == iota((32, FIELDS), 1), 1.0, 0.0).astype(F32), mixing)
    entries = jnp.where(number % FIELDS == iota((32, FIELDS), 1), entries, 0.0)
    entries = jnp.broadcast_to(jnp.sum(entries, axis=1, keepdims=True), (32, 128))
    high, middle = split(entries)
    low = (entries - high.astype(F32) - middle.astype(F32)).astype(BF16)
    level_ref[ENTRIES : ENTRIES + 32, :128] = high
    level_ref[ENTRIES : ENTRIES + 32, 128:] = middle
    level_ref[ENTRIES + 32 :, :128] = low
    level_ref[ENTRIES + 32 :, 128:] = jnp.zeros((32, 128), BF16)
    power = nt(field8, mixing)
    coupled = [nt(field8, field8), nt(power, field8)]
    for _ in range(2):
        power = nt(power, mixing)
        coupled.append(nt(power, field8))
    along = nt(nt(node8, coarse_volume) + nt(along, clift), node8)
    across = nt(nt(across, clift), node8)
    ahead = nt(nt(ahead, clift), node8)
    level = DT * coupled[1] * jnp.where(same, along, across)
    beside = DT * coupled[1] * jnp.where(same, ahead, 0.0)
    upper = (tall & 1) == 1
    below = jnp.where(upper, beside, 0.0)
    above = jnp.where(upper, 0.0, beside)
    level_level = nn(level, level)
    below_all = nn(below, jnp.concatenate([level, below, above], axis=1))
    above_all = nn(above, jnp.concatenate([level, below, above], axis=1))
    once = [level, below, above, jnp.zeros((128, 128), F32)]
    squared = [
        level_level + below_all[:, 256:] + above_all[:, 128:256],
        nn(level, below) + below_all[:, :128],
        nn(level, above) + above_all[:, :128],
        below_all[:, 128:256] + above_all[:, 256:],
    ]
    for block in range(4):
        rows = slice(block * 128, (block + 1) * 128)
        put(chain_high_ref, chain_low_ref, rows, slice(0, 128), once[block])
        put(chain_high_ref, chain_low_ref, rows, slice(128, 256), 0.5 * squared[block])

    restricting = nt(twice, nn(node8, restriction))
    prolonging = nt(node8, jnp.concatenate([prolongation] * 2, axis=0))
    down = (tall >= 64) == (((wide >> 3) & 1) == 1)
    up = (wide >= 64) == (((tall >> 3) & 1) == 1)
    restricting = jnp.where(down, restricting, 0.0)
    prolonging = jnp.where(up, prolonging, 0.0)
    for field in range(FIELDS):
        rows = slice(RESTRICT + field * 128, RESTRICT + (field + 1) * 128)
        put_packed(level_ref, rows, jnp.where((wide >> 4) == field, restricting, 0.0))
    put_packed(level_ref, slice(PROLONG, ENTRIES), prolonging)

    response = jnp.where(tall < 16, prolonging, 0.0)
    fine_below = (wide & 3) == 3
    responses = [nn(response, restricting)]
    for _ in range(3):
        near = jnp.where(fine_below, pltpu.roll(response, 16, 0), pltpu.roll(response, 112, 0))
        response = nn(jnp.concatenate([response, near], axis=1), psi)
        responses.append(nn(response, restricting))

    def block(shift, weights):
        rows = slice((shift % RING) * 16, (shift % RING) * 16 + 16)
        total = jnp.zeros((128, 128), F32)
        for order, weight in weights.items():
            if abs(shift) <= order:
                total = total + weight * coupled[order] * jnp.concatenate([responses[order][rows]] * 8, axis=0)
        return total

    kinds = [(shift, 0) for shift in SHIFTS_A] + [(shift, 1) for shift in SHIFTS_B]
    kinds += [(shift, 0) for shift in FAR_A] + [(shift, 1) for shift in FAR_B]
    ends = ({0: 1.0, 1: 2.0, 2: 1.0}, {0: 2.0, 1: 1.0})
    mid_rates = ({1: 1.0, 2: 1.0}, {1: 1.0})
    end_rates = ({1: 1.0, 2: 2.0, 3: 1.0}, {1: 2.0, 2: 1.0})
    for index, (shift, kind) in enumerate(kinds):
        rows = slice(index * 128, (index + 1) * 128)
        if index < NEAR:
            put(near_high_ref, near_low_ref, rows, slice(0, 128), block(shift, ends[kind]))
            put(near_high_ref, near_low_ref, rows, slice(128, 256), block(shift, mid_rates[kind]))
        put_packed(far_ref, rows, block(shift, end_rates[kind]))


def shifted(even, odd, shift):
    def rolled(value, by):
        return value if by == 0 else pltpu.roll(value, by % len(value), 0)

    if shift % 2 == 0:
        return rolled(even, shift // 2), rolled(odd, shift // 2)
    return rolled(odd, (shift + 1) // 2), rolled(even, (shift - 1) // 2)


def beside_layers(state, from_below, reach=1):
    half = len(state) // 2
    even, odd = state[:half], state[half:]
    below = shifted(even, odd, reach)
    above = shifted(even, odd, -reach)
    return jnp.concatenate([jnp.where(from_below, low, high) for low, high in zip(below, above)], axis=0)


def moved(state, shift):
    return jnp.concatenate(shifted(state[:LAYER], state[LAYER:], shift), axis=0)


def polynomials():
    once = np.array([1.0, 1.0])
    twice = np.polymul(once, once)
    two = np.array([1.0, 2.0])
    on_start = np.array([5 / 12, 4 / 3, 1.0])
    on_mid = np.array([2 / 3, 1 / 3, 0.0])
    on_end = np.array([-1 / 12, 1 / 3, 0.0])
    own = np.polyadd(np.polymul(on_mid, once), np.polymul(on_end, twice))
    table = {
        "first": np.polyadd(on_start, own),
        "later": np.polyadd(np.polymul(on_start, twice), own),
        "head": own,
        "push": np.polyadd(on_mid, np.polymul(on_end, two)),
        "head_before": np.polymul(on_start, twice),
        "push_before": np.polymul(on_start, two),
        "new_head": twice,
        "new_push": two,
    }
    return {name: [float(x) for x in np.pad(p[::-1], (0, 5 - len(p)))] for name, p in table.items()}


def iterate_kernel(
    slices,
    received_ref,
    level_ref,
    chain_high_ref,
    chain_low_ref,
    near_high_ref,
    near_low_ref,
    far_ref,
    sent_ref,
    mixing_ref,
    start,
    head1,
    rate1,
    head2,
    rate2,
    ends,
    ends_rate,
):
    fine_ref = level_ref.at[:256]
    mixing_ref[...] = (
        level_ref[ENTRIES : ENTRIES + 32, :128].astype(F32)
        + level_ref[ENTRIES : ENTRIES + 32, 128:].astype(F32)
        + level_ref[ENTRIES + 32 :, :128].astype(F32)
    )
    place = lax.axis_index("space")
    mine = lax.axis_index("tm")
    kx, ky, kx_other, ky_other, paired = wave_numbers(place & (UNITS - 1))
    single = paired == 0
    lane = iota((LAYER, 128), 1)
    fine_below = (lane & 3) == 3
    coarse_below = (lane & 1) == 1
    halved = lane >= 64
    of_field = iota((128, 128), 1) >> 4

    def packed_dot(value, packed):
        high, low = split(value)
        both = bdot(high, packed)
        return both[:, :128] + (both[:, 128:] + bdot(low, packed[:, :128]))

    def dot3(value, high_op, low_op):
        high, low = split(value)
        return bdot(high, high_op) + (bdot(high, low_op) + bdot(low, high_op))

    def fields_of(state):
        rows = len(state) // FIELDS
        return [state[field * rows : (field + 1) * rows] for field in range(FIELDS)]

    def psi(state):
        parts = fields_of(state)
        pieces = []
        for field in range(FIELDS):
            first = field * FIELDS
            mixed = mixing_ref[first : first + 1] * parts[0]
            for other in range(1, FIELDS):
                mixed = mixed + mixing_ref[first + other : first + other + 1] * parts[other]
            pieces.append(jnp.concatenate([mixed, beside_layers(mixed, fine_below[: len(mixed) // 2])], axis=1))
        return packed_dot(jnp.concatenate(pieces, axis=0), fine_ref[...])

    def restrict(state):
        return packed_dot(jnp.concatenate(fields_of(state), axis=1), level_ref[RESTRICT:PROLONG])

    def stages(states):
        wide = [
            jnp.concatenate(
                [state, moved(state, 1), moved(state, -1), beside_layers(state, coarse_below, 2)], axis=1
            )
            for state in states
        ]
        both = dot3(jnp.concatenate(wide, axis=0), chain_high_ref[...], chain_low_ref[...])
        both = [both[i * 128 : (i + 1) * 128] for i in range(len(states))]
        return [(part[:, :128], part[:, 128:]) for part in both]

    def in_order(column):
        begin = column if column < STATE else 2 * STATE
        own = received_ref[:, 0, begin : begin + 128]
        if column < STATE:
            other = received_ref[:, 0, STATE + column : STATE + column + 128]
        else:
            other = pltpu.roll(own, 124, 1)
        return jnp.concatenate([other[:EDGE], own, other[EDGE:]], axis=0)

    shifts = in_order(STATE)
    lower_triangle = jnp.where(iota((LAYER, LAYER), 1) < iota((LAYER, LAYER), 0), 1.0, 0.0).astype(F32)
    first_x, first_y = shifts[:, 0:1], shifts[:, 1:2]
    both_x, both_y = first_x + shifts[:, 2:3], first_y + shifts[:, 3:4]
    passed_x = nn(lower_triangle, jnp.broadcast_to(both_x, (LAYER, 128)))
    passed_y = nn(lower_triangle, jnp.broadcast_to(both_y, (LAYER, 128)))
    turning = []
    for add_x, add_y in ((first_x, first_y), (both_x, both_y)):
        shift_x = (passed_x + add_x).astype(jnp.int32)
        shift_y = (passed_y + add_y).astype(jnp.int32)
        turns = jnp.where(halved, kx_other, kx) * shift_x + jnp.where(halved, ky_other, ky) * shift_y
        cos = eighth_cos(turns)
        sin = jnp.where(single, 0.0, eighth_cos(turns - 2))
        turning.append((cos, jnp.where(halved, sin, -sin)))

    for field in range(FIELDS):
        for index in range(2):
            value = in_order((field * 2 + index) * 128)
            cos, sin = turning[index]
            begin = field * 128 + index * LAYER
            start[begin : begin + LAYER] = value * cos + pltpu.roll(value, 64, 1) * sin

    initial = start[...]
    power = psi(initial)
    begin = restrict(initial)
    power_coarse = [begin, restrict(power)]
    ((begin_rate, begin_twice),) = stages([begin])
    defect = 2.0 * power_coarse[1] - begin_rate
    head, rate = begin, begin_rate
    later_head, later_rate = begin, begin_rate
    old_rate, old_twice, last = begin_rate, begin_twice, power_coarse[1]
    head1[0], rate1[0] = begin, begin_rate
    head2[0], rate2[0] = begin, begin_rate
    ends[0], ends_rate[0] = begin, begin_rate

    def needed(change, push):
        kinds = [(shift, change) for shift in SHIFTS_A] + [(shift, push) for shift in SHIFTS_B]
        kinds += [(shift, change) for shift in FAR_A] + [(shift, push) for shift in FAR_B]
        parts = [split(moved(value, shift)) for shift, value in kinds]
        high = jnp.concatenate([part[0] for part in parts], axis=1)
        low = jnp.concatenate([part[1] for part in parts], axis=1)
        near_high, near_low = high[:, : NEAR * 128], low[:, : NEAR * 128]
        near = bdot(near_high, near_high_ref[...]) + (
            bdot(near_high, near_low_ref[...]) + bdot(near_low, near_high_ref[...])
        )
        far = bdot(high, far_ref[...])
        return near[:, :128], near[:, 128:], far[:, :128] + (far[:, 128:] + bdot(low, far_ref[:, :128]))

    previous = jnp.maximum(mine - 1, 0)
    later = jnp.where(mine > 0, 1.0, 0.0).astype(F32)
    table = polynomials()

    def around(state):
        half = len(state) // 2
        return jnp.concatenate(
            [state[EDGE - MARGIN : EDGE + UNITS + MARGIN], state[half + EDGE - MARGIN : half + EDGE + UNITS + MARGIN]],
            axis=0,
        )

    initial_around = jnp.concatenate([around(part) for part in fields_of(initial)], axis=0)

    def added(order):
        total = None
        for name, value in parts.items():
            if table[name][order] != 0.0:
                term = table[name][order] * value
                total = term if total is None else total + term
        apart = [jnp.where(of_field[: len(total)] == field, total, 0.0) for field in range(FIELDS)]
        wide = packed_dot(jnp.concatenate(apart, axis=0), level_ref[PROLONG:ENTRIES])
        weight = jnp.where(mine > 0, table["later"][order], table["first"][order]).astype(F32)
        return wide + weight * initial_around

    waiting = []
    ready = None
    for step in range(slices + 2):
        states = []
        if step < slices:
            states.append(rate + defect)
        if ready is not None:
            tail = ready[0] + end_start
            next_last = ready[2] + end_rate_start
            integral = (last + 4.0 * (ready[1] + mid_rate_start) + next_last) * (1.0 / 3.0)
            later_defect = integral - old_rate
            states += [tail, later_rate + later_defect]
        found = stages(states)
        if ready is not None:
            (tail_rate, tail_twice), (once, half_twice) = found[-2:]
            later_head = later_head + later_rate + later_defect + 0.5 * (old_rate - tail_rate + once)
            later_rate = later_rate + once + half_twice + (old_twice - tail_twice)
            old_rate, old_twice, last = tail_rate, tail_twice, next_last
            slot = step - 1
            head2[slot], rate2[slot] = later_head, later_rate
            ends[slot], ends_rate[slot] = tail, tail_rate
        ready = needed(*waiting.pop()) if waiting else None
        if step < slices:
            once, half_twice = found[0]
            change = head - begin
            head, next_rate = head + rate + defect + 0.5 * once, rate + once + half_twice
            waiting.append((change, (next_rate - rate) * 0.125))
            rate = next_rate
            head1[step + 1], rate1[step + 1] = head, rate
        if step == slices - 1:
            parts = {
                "head": around(head1[mine] - begin),
                "push": around((rate1[mine + 1] - rate1[mine]) * 0.125),
                "head_before": around((head1[previous] - begin) * later),
                "push_before": around((rate1[mine] - rate1[previous]) * (0.125 * later)),
            }
            state = added(4)
            state = psi(state) + added(3)
        if step < 2:
            power = psi(power)
            power_coarse.append(restrict(power))
        if step == 1:
            end_start = power_coarse[0] + 2.0 * power_coarse[1] + power_coarse[2]
            mid_rate_start = power_coarse[1] + power_coarse[2]
            end_rate_start = power_coarse[1] + 2.0 * power_coarse[2] + power_coarse[3]

    new_head = head2[mine] - ends[mine]
    new_push = ((rate2[mine + 1] - ends_rate[mine + 1]) - (rate2[mine] - ends_rate[mine])) * 0.125
    parts["new_head"], parts["new_push"] = around(new_head), around(new_push)
    for order in (2, 1, 0):
        state = psi(state) + added(order)
    turned = [(cos[EDGE - MARGIN : EDGE + UNITS + MARGIN], sin[EDGE - MARGIN : EDGE + UNITS + MARGIN]) for cos, sin in turning]
    rows = len(state) // (2 * FIELDS)
    for field in range(FIELDS):
        for index in range(2):
            cos, sin = turned[index]
            begin_row = (field * 2 + index) * rows
            value = state[begin_row : begin_row + rows]
            value = value * cos - pltpu.roll(value, 64, 1) * sin
            column = (field * 2 + index) * 128
            sent_ref[:, 0, column : column + 128] = value[MARGIN : MARGIN + UNITS]


IN_VMEM = pl.BlockSpec(memory_space=pltpu.VMEM)


def operators_call(volume_op, lift_op, coarse_volume, coarse_lift, mixing, restrict_op, prolong_op):
    shapes = [
        (ENTRIES + 64, 256),
        (512, 256),
        (512, 256),
        (NEAR * 128, 256),
        (NEAR * 128, 256),
        (BLOCKS * 128, 256),
    ]
    operands = (volume_op, lift_op, coarse_volume, coarse_lift, mixing, restrict_op, prolong_op)
    packed = jnp.zeros((224, 128), F32)
    for operand, (first, rows, columns) in zip(operands, PACKED):
        packed = packed + jnp.pad(operand, ((first, 224 - first - rows), (0, 128 - columns)))
    return pl.pallas_call(
        operators_kernel,
        out_shape=[jax.ShapeDtypeStruct(shape, BF16) for shape in shapes],
        in_specs=[IN_VMEM],
        out_specs=[IN_VMEM] * len(shapes),
        compiler_params=pltpu.CompilerParams(vmem_limit_bytes=VMEM_LIMIT),
        cost_estimate=pl.CostEstimate(flops=10**8, bytes_accessed=3 * 10**6, transcendentals=0),
        name="operators",
    )(packed)


def iterate_kernel_call(slices, received, operators):
    coarse_shape = pltpu.VMEM((slices + 1, 128, 128), F32)
    return pl.pallas_call(
        functools.partial(iterate_kernel, slices),
        out_shape=jax.ShapeDtypeStruct((UNITS, 1, STATE), F32),
        in_specs=[IN_VMEM] * (1 + len(operators)),
        out_specs=IN_VMEM,
        scratch_shapes=[pltpu.VMEM((32, 128), F32), pltpu.VMEM((FIELDS * 128, 128), F32)]
        + [coarse_shape] * 6,
        compiler_params=pltpu.CompilerParams(vmem_limit_bytes=VMEM_LIMIT),
        name="iterate",
    )(received, *operators)


def iterate_call(slices, received, volume_op, lift_op, coarse_volume, coarse_lift, mixing, restrict_op, prolong_op):
    operators = operators_call(
        volume_op, lift_op, coarse_volume, coarse_lift, mixing, restrict_op, prolong_op
    )
    return iterate_kernel_call(slices, received[:, None, :], operators)


def window_partners(slices, places):
    per_chip_row = 8
    depth = places // per_chip_row
    ring = 2 * depth
    route = []
    for slot in range(slices):
        for place in range(places):
            z = slot % 2 * depth + place // per_chip_row
            other = (z - 2 if z % 4 < 2 else z + 2) % ring
            partner = (slot - slot % 2 + other // depth) * places + other % depth * per_chip_row
            route.append((partner + place % per_chip_row, slot * places + place))
    return route


def on_device(
    initial,
    neighbours,
    volume_op,
    lift_op,
    coarse_volume,
    coarse_lift,
    mixing,
    restrict_op,
    prolong_op,
):
    params = pltpu.CompilerParams(vmem_limit_bytes=VMEM_LIMIT)
    route = window_partners(lax.axis_size("tm"), lax.axis_size("space"))
    state = initial.reshape(FIELDS * LAYER, -1)
    state_beside = lax.ppermute(state, ("tm", "space"), route)
    links_beside = lax.ppermute(neighbours, ("tm", "space"), route)
    block_shape = jax.ShapeDtypeStruct((UNITS, 1, 2 * STATE + 128), F32)
    half, basis = pl.pallas_call(
        own_modes_kernel,
        out_shape=(block_shape, jax.ShapeDtypeStruct((LAYER + 8, 128), F32)),
        in_specs=[IN_VMEM] * 2,
        out_specs=(pl.BlockSpec(memory_space=pl.ANY), IN_VMEM),
        scratch_shapes=[pltpu.VMEM((UNITS, 1, STATE), F32), pltpu.SemaphoreType.DMA],
        compiler_params=params,
        name="own_modes",
    )(state, neighbours)
    sent = pl.pallas_call(
        beside_modes_kernel,
        out_shape=block_shape,
        in_specs=[pl.BlockSpec(memory_space=pl.ANY)] + [IN_VMEM] * 3,
        out_specs=pl.BlockSpec(memory_space=pl.ANY),
        input_output_aliases={0: 0},
        scratch_shapes=[pltpu.VMEM((UNITS, 1, STATE + 128), F32), pltpu.SemaphoreType.DMA((FIELDS + 1,))],
        compiler_params=params,
        name="beside_modes",
    )(half, basis, state_beside, links_beside)
    windows = [[first + i for i in range(UNITS)] for first in range(0, lax.axis_size("space"), UNITS)]

    def exchange(blocks):
        return lax.all_to_all(blocks, "space", 0, 0, axis_index_groups=windows, tiled=True)

    received = exchange(sent)
    operators = operators_call(
        volume_op, lift_op, coarse_volume, coarse_lift, mixing, restrict_op, prolong_op
    )
    modes = iterate_kernel_call(lax.axis_size("tm"), received, operators)
    returned = exchange(modes)
    return pl.pallas_call(
        from_modes_kernel,
        out_shape=jax.ShapeDtypeStruct((1, FIELDS, LAYER, 128), F32),
        in_specs=[IN_VMEM] * 2,
        out_specs=pl.BlockSpec(memory_space=pl.ANY),
        scratch_shapes=[pltpu.VMEM((FIELDS, LAYER, 128), F32), pltpu.SemaphoreType.DMA((FIELDS,))],
        compiler_params=params,
        name="from_modes",
    )(returned, basis)


def solution(mesh):
    return jax.shard_map(
        on_device,
        mesh=mesh,
        in_specs=(P(None, None, "space"), P(None, "space"), P(), P(), P(), P(), P(), P(), P()),
        out_specs=P("tm", None, None, "space"),
        check_vma=False,
    )
```

```python
import functools

import jax
import jax.numpy as jnp
import numpy as np
from jax import lax
from jax.experimental import pallas as pl
from jax.experimental.pallas import tpu as pltpu
from jax.sharding import PartitionSpec as P

LAYER = 64
FIELDS = 5
DT = 0.125
HALF = 0.7071067811865476
UNITS = 32
STATE = FIELDS * 2 * 128
EDGE = 16
MARGIN = 8
EXACT = lax.Precision.HIGHEST
F32 = jnp.float32
BF16 = jnp.bfloat16
VMEM_LIMIT = 20 * 1024 * 1024


def iota(shape, dim):
    return lax.broadcasted_iota(jnp.int32, shape, dim)


def nn(a, b):
    return lax.dot_general(a, b, (((1,), (0,)), ((), ())), precision=EXACT, preferred_element_type=F32)


def nt(a, b):
    return lax.dot_general(a, b, (((1,), (1,)), ((), ())), precision=EXACT, preferred_element_type=F32)


def nt3(a, b):
    dims = (((1,), (1,)), ((), ()))
    return lax.dot_general(a, b, dims, precision=lax.Precision.HIGH, preferred_element_type=F32)


def nn3(a, b):
    dims = (((1,), (0,)), ((), ()))
    return lax.dot_general(a, b, dims, precision=lax.Precision.HIGH, preferred_element_type=F32)


def eighth_cos(turn):
    turn = turn & 7
    diagonal = jnp.where((turn == 1) | (turn == 7), HALF, jnp.where((turn == 3) | (turn == 5), -HALF, 0.0))
    return jnp.where(turn == 0, 1.0, jnp.where(turn == 4, -1.0, diagonal)).astype(F32)


def wave_numbers(unit):
    low = unit - 23
    high = unit - 26
    kx = jnp.where(unit < 24, unit & 7, jnp.where(unit < 27, low, jnp.where(unit < 30, high, 0)))
    ky = jnp.where(unit < 24, 1 + (unit >> 3), jnp.where(unit < 27, 0, jnp.where(unit == 30, 0, 4)))
    paired = jnp.where(unit < 30, 1, 0)
    kx_other = jnp.where(unit < 30, kx, 4)
    return kx, ky, kx_other, ky, paired


def grid_places(links, base, total, first_slot):
    lane = iota((1, 128), 1)
    upper = lane >= LAYER
    target = iota((128, 128), 0)

    def steps(face):
        one = jnp.where(links[face : face + 1] - base == target, 1.0, 0.0).astype(BF16)
        two = jnp.dot(one, one, preferred_element_type=F32).astype(BF16)
        four = jnp.dot(two, two, preferred_element_type=F32).astype(BF16)
        return one, two, four

    row = iota((8, 128), 0)
    found = jnp.where((row == 0) & ((iota((8, 128), 1) & (LAYER - 1)) == 0), 1.0, 0.0).astype(F32)
    for part, moves in ((1, steps(0)), (2, steps(2))):
        for power, move in enumerate(moves):
            shifted = jnp.dot(found.astype(BF16), move, preferred_element_type=F32)
            found = found + shifted + jnp.where(row == part, shifted[0:1] * (1 << power), 0.0)
    along_x = found[1:2]
    along_y = found[2:3]

    below = jnp.where(upper, base, (base + total - LAYER) % total)
    hit = links[4:5] == below
    extra = jnp.zeros((1, 128), F32)
    for slot, (layer_upper, value) in enumerate(
        ((False, along_x), (False, along_y), (True, along_x), (True, along_y))
    ):
        part = jnp.where(hit & (upper == layer_upper), value, 0.0)
        extra = jnp.where(lane == first_slot + slot, jnp.sum(part, axis=1, keepdims=True), extra)
    return along_x.astype(jnp.int32), along_y.astype(jnp.int32), extra


def layer_modes(ref, links, where, places, first_slot):
    upper = iota((1, 128), 1) >= LAYER
    halved = iota((UNITS, 128), 1) >= LAYER
    mode = iota((LAYER, 128), 0)
    kx, ky, kx_other, ky_other, paired = wave_numbers(mode & (UNITS - 1))
    second = mode >= UNITS
    along_x, along_y, extra = grid_places(links, where * 2 * LAYER, places * 2 * LAYER, first_slot)
    turns = jnp.where(second, kx_other, kx) * along_x + jnp.where(second, ky_other, ky) * along_y
    basis = eighth_cos(turns + jnp.where(second, 2 * paired, 0))
    apart = jnp.concatenate([jnp.where(upper, 0.0, basis), jnp.where(upper, basis, 0.0)], axis=0)

    def of_field(field):
        state = ref[field * LAYER : (field + 1) * LAYER]
        modes = nt3(apart, jnp.concatenate([state, state], axis=0))
        return [
            jnp.where(
                halved,
                modes[index * LAYER + UNITS : (index + 1) * LAYER],
                modes[index * LAYER : index * LAYER + UNITS],
            )
            for index in range(2)
        ]

    return basis, of_field, extra


def own_modes_kernel(own_ref, links_ref, sent_ref, basis_ref, blocks, semaphore):
    basis, modes_of, extra = layer_modes(own_ref, links_ref[...], lax.axis_index("space"), lax.axis_size("space"), 0)
    for field in range(FIELDS):
        for index, value in enumerate(modes_of(field)):
            column = (field * 2 + index) * 128
            blocks[:, 0, column : column + 128] = value
    copy = pltpu.make_async_copy(blocks, sent_ref.at[:, :, :STATE], semaphore)
    copy.start()
    basis_ref[:LAYER] = basis
    basis_ref[LAYER:] = jnp.broadcast_to(extra, (8, 128))
    copy.wait()


def beside_modes_kernel(half_ref, basis_ref, beside_ref, links_ref, sent_ref, blocks, semaphores):
    del half_ref
    place = lax.axis_index("space")
    places = lax.axis_size("space")
    partner = (jnp.where(((place >> 3) & 3) < 2, place - EDGE, place + EDGE) + places) % places
    copies = []

    def send(first, columns):
        part = pltpu.make_async_copy(
            blocks.at[:, :, first : first + columns],
            sent_ref.at[:, :, STATE + first : STATE + first + columns],
            semaphores.at[len(copies)],
        )
        part.start()
        copies.append(part)

    _, modes_of, extra = layer_modes(beside_ref, links_ref[...], partner, places, 4)
    for field in range(FIELDS):
        for index, value in enumerate(modes_of(field)):
            column = (field * 2 + index) * 128
            blocks[:, 0, column : column + 128] = value
        send(field * 256, 256)
    blocks[:, 0, STATE:] = jnp.broadcast_to(basis_ref[LAYER : LAYER + 1] + extra, (UNITS, 128))
    send(STATE, 128)
    for copy in copies:
        copy.wait()


def from_modes_kernel(modes_ref, basis_ref, out_ref, fields, semaphores):
    copies = []
    unit = iota((LAYER, 128), 0) & (UNITS - 1)
    scale = jnp.where(unit < 30, 2.0 / LAYER, 1.0 / LAYER).astype(F32)
    back = basis_ref[:LAYER] * scale
    upper = iota((LAYER, 128), 1) >= LAYER
    halved = iota((UNITS, 128), 1) >= LAYER
    for field in range(FIELDS):
        column = field * 256
        even = modes_ref[:, 0, column : column + 128]
        odd = modes_ref[:, 0, column + 128 : column + 256]
        real = jnp.where(halved, pltpu.roll(odd, 64, 1), even)
        imaginary = jnp.where(halved, odd, pltpu.roll(even, 64, 1))
        whole = nn3(jnp.transpose(jnp.concatenate([real, imaginary], axis=0)), back)
        fields[field] = jnp.where(upper, whole[LAYER:], whole[:LAYER])
        copies.append(pltpu.make_async_copy(fields.at[field], out_ref.at[0, field], semaphores.at[field]))
        copies[-1].start()
    for copy in copies:
        copy.wait()


SHIFTS_A = (0, 1, -1, 2, -2)
SHIFTS_B = (0, 1, -1)
FAR_A = (3, -3)
FAR_B = (2, -2)
NEAR = len(SHIFTS_A) + len(SHIFTS_B)
BLOCKS = NEAR + len(FAR_A) + len(FAR_B)
RING = 8
RESTRICT = 256
PROLONG = RESTRICT + FIELDS * 128
ENTRIES = PROLONG + 128
PACKED = ((0, 64, 64), (64, 64, 96), (128, 8, 8), (136, 8, 24), (144, FIELDS, FIELDS), (152, 8, 64), (160, 64, 8))


def face_weights(shape, per_edge, node, weights):
    column = iota(shape, 1)
    face = column // (per_edge * per_edge)
    trace = column % (per_edge * per_edge)
    a, b, c = (node // (per_edge * per_edge), (node // per_edge) % per_edge, node % per_edge)
    first = [a, a, b, b, c, c]
    rest = [b * per_edge + c] * 2 + [a * per_edge + c] * 2 + [a * per_edge + b] * 2
    result = jnp.zeros(shape, F32)
    for which, weight in weights.items():
        edge = per_edge - 1 if which % 2 == 0 else 0
        on = (face == which) & (first[which] == edge) & (rest[which] == trace)
        result = jnp.where(on, weight, result)
    return result


def split(value):
    high = value.astype(BF16)
    return high, (value - high.astype(F32)).astype(BF16)


def bdot(a, b):
    return jnp.dot(a, b, preferred_element_type=F32)


def operators_kernel(
    packed_ref,
    level_ref,
    chain_high_ref,
    chain_low_ref,
    near_high_ref,
    near_low_ref,
    far_ref,
):
    volume, lift, coarse_volume, clift, mixing, restriction, prolongation = (
        packed_ref[first : first + rows, :columns] for first, rows, columns in PACKED
    )
    fine_ref = level_ref.at[:256]
    place = lax.axis_index("space")
    kx, ky, kx_other, ky_other, paired = wave_numbers(place & (UNITS - 1))
    single = paired == 0

    def turn_cos(first, second, second_half):
        return jnp.where(second_half, eighth_cos(second), eighth_cos(first))

    def put_packed(ref, rows, value):
        high, low = split(value)
        ref[rows, :128] = high
        ref[rows, 128:] = low

    def put(high_ref, low_ref, rows, columns, value):
        high, low = split(value)
        high_ref[rows, columns] = high
        low_ref[rows, columns] = low

    wide = iota((128, 128), 1)
    tall = iota((128, 128), 0)
    row = iota((128, 96), 0)
    half = row >= 64
    same = (wide >= 64) == (tall >= 64)
    cos_x = turn_cos(kx, kx_other, half)
    cos_y = turn_cos(ky, ky_other, half)
    sin_x = jnp.where(single, 0.0, eighth_cos(kx - 2))
    sin_y = jnp.where(single, 0.0, eighth_cos(ky - 2))
    sign = jnp.where(half, -1.0, 1.0)
    along = face_weights((128, 96), 4, row & 63, {0: cos_x, 1: cos_x, 2: cos_y, 3: cos_y})
    across = face_weights(
        (128, 96), 4, row & 63, {0: -sin_x * sign, 1: sin_x * sign, 2: -sin_y * sign, 3: sin_y * sign}
    )
    ahead = face_weights((128, 96), 4, row & 63, {4: 1.0, 5: 1.0})
    lift2 = jnp.concatenate([lift] * 2, axis=0)
    volume2 = jnp.concatenate([volume] * 2, axis=0)
    twice = jnp.where((iota((128, 64), 0) & 63) == iota((128, 64), 1), 1.0, 0.0).astype(F32)
    inside = (DT / 2) * jnp.where(same, nt(twice, volume2) + nt(along, lift2), nt(across, lift2))
    beside = (DT / 2) * jnp.where(same, nt(ahead, lift2), 0.0)
    put_packed(fine_ref, slice(0, 128), inside)
    put_packed(fine_ref, slice(128, 256), beside)
    psi = jnp.concatenate([inside, beside], axis=0)

    row = iota((128, 24), 0)
    half = ((row >> 3) & 1) == 1
    cos_x = turn_cos(kx, kx_other, half)
    cos_y = turn_cos(ky, ky_other, half)
    sign = jnp.where(half, -1.0, 1.0)
    along = face_weights((128, 24), 2, row & 7, {0: cos_x, 1: cos_x, 2: cos_y, 3: cos_y})
    across = face_weights(
        (128, 24), 2, row & 7, {0: -sin_x * sign, 1: sin_x * sign, 2: -sin_y * sign, 3: sin_y * sign}
    )
    ahead = face_weights((128, 24), 2, row & 7, {4: 1.0, 5: 1.0})
    node8 = jnp.where((iota((128, 8), 0) & 7) == iota((128, 8), 1), 1.0, 0.0).astype(F32)
    field8 = jnp.where((iota((128, FIELDS), 0) >> 4) == iota((128, FIELDS), 1), 1.0, 0.0).astype(F32)
    same = ((wide >> 3) & 1) == ((tall >> 3) & 1)
    number = iota((32, FIELDS), 0)
    entries = nn(jnp.where(number // FIELDS == iota((32, FIELDS), 1), 1.0, 0.0).astype(F32), mixing)
    entries = jnp.where(number % FIELDS == iota((32, FIELDS), 1), entries, 0.0)
    entries = jnp.broadcast_to(jnp.sum(entries, axis=1, keepdims=True), (32, 128))
    high, middle = split(entries)
    low = (entries - high.astype(F32) - middle.astype(F32)).astype(BF16)
    level_ref[ENTRIES : ENTRIES + 32, :128] = high
    level_ref[ENTRIES : ENTRIES + 32, 128:] = middle
    level_ref[ENTRIES + 32 :, :128] = low
    level_ref[ENTRIES + 32 :, 128:] = jnp.zeros((32, 128), BF16)
    power = nt(field8, mixing)
    coupled = [nt(field8, field8), nt(power, field8)]
    for _ in range(2):
        power = nt(power, mixing)
        coupled.append(nt(power, field8))
    along = nt(nt(node8, coarse_volume) + nt(along, clift), node8)
    across = nt(nt(across, clift), node8)
    ahead = nt(nt(ahead, clift), node8)
    level = DT * coupled[1] * jnp.where(same, along, across)
    beside = DT * coupled[1] * jnp.where(same, ahead, 0.0)
    upper = (tall & 1) == 1
    below = jnp.where(upper, beside, 0.0)
    above = jnp.where(upper, 0.0, beside)
    level_level = nn(level, level)
    below_all = nn(below, jnp.concatenate([level, below, above], axis=1))
    above_all = nn(above, jnp.concatenate([level, below, above], axis=1))
    once = [level, below, above, jnp.zeros((128, 128), F32)]
    squared = [
        level_level + below_all[:, 256:] + above_all[:, 128:256],
        nn(level, below) + below_all[:, :128],
        nn(level, above) + above_all[:, :128],
        below_all[:, 128:256] + above_all[:, 256:],
    ]
    for block in range(4):
        rows = slice(block * 128, (block + 1) * 128)
        put(chain_high_ref, chain_low_ref, rows, slice(0, 128), once[block])
        put(chain_high_ref, chain_low_ref, rows, slice(128, 256), 0.5 * squared[block])

    restricting = nt(twice, nn(node8, restriction))
    prolonging = nt(node8, jnp.concatenate([prolongation] * 2, axis=0))
    down = (tall >= 64) == (((wide >> 3) & 1) == 1)
    up = (wide >= 64) == (((tall >> 3) & 1) == 1)
    restricting = jnp.where(down, restricting, 0.0)
    prolonging = jnp.where(up, prolonging, 0.0)
    for field in range(FIELDS):
        rows = slice(RESTRICT + field * 128, RESTRICT + (field + 1) * 128)
        put_packed(level_ref, rows, jnp.where((wide >> 4) == field, restricting, 0.0))
    put_packed(level_ref, slice(PROLONG, ENTRIES), prolonging)

    response = jnp.where(tall < 16, prolonging, 0.0)
    fine_below = (wide & 3) == 3
    responses = [nn(response, restricting)]
    for _ in range(3):
        near = jnp.where(fine_below, pltpu.roll(response, 16, 0), pltpu.roll(response, 112, 0))
        response = nn(jnp.concatenate([response, near], axis=1), psi)
        responses.append(nn(response, restricting))

    def block(shift, weights):
        rows = slice((shift % RING) * 16, (shift % RING) * 16 + 16)
        total = jnp.zeros((128, 128), F32)
        for order, weight in weights.items():
            if abs(shift) <= order:
                total = total + weight * coupled[order] * jnp.concatenate([responses[order][rows]] * 8, axis=0)
        return total

    kinds = [(shift, 0) for shift in SHIFTS_A] + [(shift, 1) for shift in SHIFTS_B]
    kinds += [(shift, 0) for shift in FAR_A] + [(shift, 1) for shift in FAR_B]
    ends = ({0: 1.0, 1: 2.0, 2: 1.0}, {0: 2.0, 1: 1.0})
    mid_rates = ({1: 1.0, 2: 1.0}, {1: 1.0})
    end_rates = ({1: 1.0, 2: 2.0, 3: 1.0}, {1: 2.0, 2: 1.0})
    for index, (shift, kind) in enumerate(kinds):
        rows = slice(index * 128, (index + 1) * 128)
        if index < NEAR:
            put(near_high_ref, near_low_ref, rows, slice(0, 128), block(shift, ends[kind]))
            put(near_high_ref, near_low_ref, rows, slice(128, 256), block(shift, mid_rates[kind]))
        put_packed(far_ref, rows, block(shift, end_rates[kind]))


def shifted(even, odd, shift):
    def rolled(value, by):
        return value if by == 0 else pltpu.roll(value, by % len(value), 0)

    if shift % 2 == 0:
        return rolled(even, shift // 2), rolled(odd, shift // 2)
    return rolled(odd, (shift + 1) // 2), rolled(even, (shift - 1) // 2)


def beside_layers(state, from_below, reach=1):
    half = len(state) // 2
    even, odd = state[:half], state[half:]
    below = shifted(even, odd, reach)
    above = shifted(even, odd, -reach)
    return jnp.concatenate([jnp.where(from_below, low, high) for low, high in zip(below, above)], axis=0)


def moved(state, shift):
    return jnp.concatenate(shifted(state[:LAYER], state[LAYER:], shift), axis=0)


def polynomials():
    once = np.array([1.0, 1.0])
    twice = np.polymul(once, once)
    two = np.array([1.0, 2.0])
    on_start = np.array([5 / 12, 4 / 3, 1.0])
    on_mid = np.array([2 / 3, 1 / 3, 0.0])
    on_end = np.array([-1 / 12, 1 / 3, 0.0])
    own = np.polyadd(np.polymul(on_mid, once), np.polymul(on_end, twice))
    table = {
        "first": np.polyadd(on_start, own),
        "later": np.polyadd(np.polymul(on_start, twice), own),
        "head": own,
        "push": np.polyadd(on_mid, np.polymul(on_end, two)),
        "head_before": np.polymul(on_start, twice),
        "push_before": np.polymul(on_start, two),
        "new_head": twice,
        "new_push": two,
    }
    return {name: [float(x) for x in np.pad(p[::-1], (0, 5 - len(p)))] for name, p in table.items()}


def iterate_kernel(
    slices,
    received_ref,
    level_ref,
    chain_high_ref,
    chain_low_ref,
    near_high_ref,
    near_low_ref,
    far_ref,
    sent_ref,
    mixing_ref,
    start,
    head1,
    rate1,
    head2,
    rate2,
    ends,
    ends_rate,
):
    fine_ref = level_ref.at[:256]
    mixing_ref[...] = (
        level_ref[ENTRIES : ENTRIES + 32, :128].astype(F32)
        + level_ref[ENTRIES : ENTRIES + 32, 128:].astype(F32)
        + level_ref[ENTRIES + 32 :, :128].astype(F32)
    )
    place = lax.axis_index("space")
    mine = lax.axis_index("tm")
    kx, ky, kx_other, ky_other, paired = wave_numbers(place & (UNITS - 1))
    single = paired == 0
    lane = iota((LAYER, 128), 1)
    fine_below = (lane & 3) == 3
    coarse_below = (lane & 1) == 1
    halved = lane >= 64
    of_field = iota((128, 128), 1) >> 4

    def packed_dot(value, packed):
        high, low = split(value)
        both = bdot(high, packed)
        return both[:, :128] + (both[:, 128:] + bdot(low, packed[:, :128]))

    def dot3(value, high_op, low_op):
        high, low = split(value)
        return bdot(high, high_op) + (bdot(high, low_op) + bdot(low, high_op))

    def fields_of(state):
        rows = len(state) // FIELDS
        return [state[field * rows : (field + 1) * rows] for field in range(FIELDS)]

    def psi(state):
        parts = fields_of(state)
        pieces = []
        for field in range(FIELDS):
            first = field * FIELDS
            mixed = mixing_ref[first : first + 1] * parts[0]
            for other in range(1, FIELDS):
                mixed = mixed + mixing_ref[first + other : first + other + 1] * parts[other]
            pieces.append(jnp.concatenate([mixed, beside_layers(mixed, fine_below[: len(mixed) // 2])], axis=1))
        return packed_dot(jnp.concatenate(pieces, axis=0), fine_ref[...])

    def restrict(state):
        return packed_dot(jnp.concatenate(fields_of(state), axis=1), level_ref[RESTRICT:PROLONG])

    def stages(states):
        wide = [
            jnp.concatenate(
                [state, moved(state, 1), moved(state, -1), beside_layers(state, coarse_below, 2)], axis=1
            )
            for state in states
        ]
        both = dot3(jnp.concatenate(wide, axis=0), chain_high_ref[...], chain_low_ref[...])
        both = [both[i * 128 : (i + 1) * 128] for i in range(len(states))]
        return [(part[:, :128], part[:, 128:]) for part in both]

    def in_order(column):
        begin = column if column < STATE else 2 * STATE
        own = received_ref[:, 0, begin : begin + 128]
        if column < STATE:
            other = received_ref[:, 0, STATE + column : STATE + column + 128]
        else:
            other = pltpu.roll(own, 124, 1)
        return jnp.concatenate([other[:EDGE], own, other[EDGE:]], axis=0)

    shifts = in_order(STATE)
    lower_triangle = jnp.where(iota((LAYER, LAYER), 1) < iota((LAYER, LAYER), 0), 1.0, 0.0).astype(F32)
    first_x, first_y = shifts[:, 0:1], shifts[:, 1:2]
    both_x, both_y = first_x + shifts[:, 2:3], first_y + shifts[:, 3:4]
    passed_x = nn(lower_triangle, jnp.broadcast_to(both_x, (LAYER, 128)))
    passed_y = nn(lower_triangle, jnp.broadcast_to(both_y, (LAYER, 128)))
    turning = []
    for add_x, add_y in ((first_x, first_y), (both_x, both_y)):
        shift_x = (passed_x + add_x).astype(jnp.int32)
        shift_y = (passed_y + add_y).astype(jnp.int32)
        turns = jnp.where(halved, kx_other, kx) * shift_x + jnp.where(halved, ky_other, ky) * shift_y
        cos = eighth_cos(turns)
        sin = jnp.where(single, 0.0, eighth_cos(turns - 2))
        turning.append((cos, jnp.where(halved, sin, -sin)))

    for field in range(FIELDS):
        for index in range(2):
            value = in_order((field * 2 + index) * 128)
            cos, sin = turning[index]
            begin = field * 128 + index * LAYER
            start[begin : begin + LAYER] = value * cos + pltpu.roll(value, 64, 1) * sin

    initial = start[...]
    power = psi(initial)
    begin = restrict(initial)
    power_coarse = [begin, restrict(power)]
    ((begin_rate, begin_twice),) = stages([begin])
    defect = 2.0 * power_coarse[1] - begin_rate
    head, rate = begin, begin_rate
    later_head, later_rate = begin, begin_rate
    old_rate, old_twice, last = begin_rate, begin_twice, power_coarse[1]
    head1[0], rate1[0] = begin, begin_rate
    head2[0], rate2[0] = begin, begin_rate
    ends[0], ends_rate[0] = begin, begin_rate

    def needed(change, push):
        kinds = [(shift, change) for shift in SHIFTS_A] + [(shift, push) for shift in SHIFTS_B]
        kinds += [(shift, change) for shift in FAR_A] + [(shift, push) for shift in FAR_B]
        parts = [split(moved(value, shift)) for shift, value in kinds]
        high = jnp.concatenate([part[0] for part in parts], axis=1)
        low = jnp.concatenate([part[1] for part in parts], axis=1)
        near_high, near_low = high[:, : NEAR * 128], low[:, : NEAR * 128]
        near = bdot(near_high, near_high_ref[...]) + (
            bdot(near_high, near_low_ref[...]) + bdot(near_low, near_high_ref[...])
        )
        far = bdot(high, far_ref[...])
        return near[:, :128], near[:, 128:], far[:, :128] + (far[:, 128:] + bdot(low, far_ref[:, :128]))

    previous = jnp.maximum(mine - 1, 0)
    later = jnp.where(mine > 0, 1.0, 0.0).astype(F32)
    table = polynomials()

    def around(state):
        half = len(state) // 2
        return jnp.concatenate(
            [state[EDGE - MARGIN : EDGE + UNITS + MARGIN], state[half + EDGE - MARGIN : half + EDGE + UNITS + MARGIN]],
            axis=0,
        )

    initial_around = jnp.concatenate([around(part) for part in fields_of(initial)], axis=0)

    def added(order):
        total = None
        for name, value in parts.items():
            if table[name][order] != 0.0:
                term = table[name][order] * value
                total = term if total is None else total + term
        apart = [jnp.where(of_field[: len(total)] == field, total, 0.0) for field in range(FIELDS)]
        wide = packed_dot(jnp.concatenate(apart, axis=0), level_ref[PROLONG:ENTRIES])
        weight = jnp.where(mine > 0, table["later"][order], table["first"][order]).astype(F32)
        return wide + weight * initial_around

    waiting = []
    ready = None
    for step in range(slices + 2):
        states = []
        if step < slices:
            states.append(rate + defect)
        if ready is not None:
            tail = ready[0] + end_start
            next_last = ready[2] + end_rate_start
            integral = (last + 4.0 * (ready[1] + mid_rate_start) + next_last) * (1.0 / 3.0)
            later_defect = integral - old_rate
            states += [tail, later_rate + later_defect]
        if step < 2:
            power = psi(power)
            power_coarse.append(restrict(power))
        found = stages(states)
        if ready is not None:
            (tail_rate, tail_twice), (once, half_twice) = found[-2:]
            later_head = later_head + later_rate + later_defect + 0.5 * (old_rate - tail_rate + once)
            later_rate = later_rate + once + half_twice + (old_twice - tail_twice)
            old_rate, old_twice, last = tail_rate, tail_twice, next_last
            slot = step - 1
            head2[slot], rate2[slot] = later_head, later_rate
            ends[slot], ends_rate[slot] = tail, tail_rate
        ready = needed(*waiting.pop()) if waiting else None
        if step < slices:
            once, half_twice = found[0]
            change = head - begin
            head, next_rate = head + rate + defect + 0.5 * once, rate + once + half_twice
            waiting.append((change, (next_rate - rate) * 0.125))
            rate = next_rate
            head1[step + 1], rate1[step + 1] = head, rate
        if step == slices - 1:
            parts = {
                "head": around(head1[mine] - begin),
                "push": around((rate1[mine + 1] - rate1[mine]) * 0.125),
                "head_before": around((head1[previous] - begin) * later),
                "push_before": around((rate1[mine] - rate1[previous]) * (0.125 * later)),
            }
            state = added(4)
            state = psi(state) + added(3)
        if step == 1:
            end_start = power_coarse[0] + 2.0 * power_coarse[1] + power_coarse[2]
            mid_rate_start = power_coarse[1] + power_coarse[2]
            end_rate_start = power_coarse[1] + 2.0 * power_coarse[2] + power_coarse[3]

    new_head = head2[mine] - ends[mine]
    new_push = ((rate2[mine + 1] - ends_rate[mine + 1]) - (rate2[mine] - ends_rate[mine])) * 0.125
    parts["new_head"], parts["new_push"] = around(new_head), around(new_push)
    for order in (2, 1, 0):
        state = psi(state) + added(order)
    turned = [(cos[EDGE - MARGIN : EDGE + UNITS + MARGIN], sin[EDGE - MARGIN : EDGE + UNITS + MARGIN]) for cos, sin in turning]
    rows = len(state) // (2 * FIELDS)
    for field in range(FIELDS):
        for index in range(2):
            cos, sin = turned[index]
            begin_row = (field * 2 + index) * rows
            value = state[begin_row : begin_row + rows]
            value = value * cos - pltpu.roll(value, 64, 1) * sin
            column = (field * 2 + index) * 128
            sent_ref[:, 0, column : column + 128] = value[MARGIN : MARGIN + UNITS]


IN_VMEM = pl.BlockSpec(memory_space=pltpu.VMEM)


def operators_call(volume_op, lift_op, coarse_volume, coarse_lift, mixing, restrict_op, prolong_op):
    shapes = [
        (ENTRIES + 64, 256),
        (512, 256),
        (512, 256),
        (NEAR * 128, 256),
        (NEAR * 128, 256),
        (BLOCKS * 128, 256),
    ]
    operands = (volume_op, lift_op, coarse_volume, coarse_lift, mixing, restrict_op, prolong_op)
    packed = jnp.zeros((224, 128), F32)
    for operand, (first, rows, columns) in zip(operands, PACKED):
        packed = packed + jnp.pad(operand, ((first, 224 - first - rows), (0, 128 - columns)))
    return pl.pallas_call(
        operators_kernel,
        out_shape=[jax.ShapeDtypeStruct(shape, BF16) for shape in shapes],
        in_specs=[IN_VMEM],
        out_specs=[IN_VMEM] * len(shapes),
        compiler_params=pltpu.CompilerParams(vmem_limit_bytes=VMEM_LIMIT),
        cost_estimate=pl.CostEstimate(flops=10**8, bytes_accessed=3 * 10**6, transcendentals=0),
        name="operators",
    )(packed)


def iterate_kernel_call(slices, received, operators):
    coarse_shape = pltpu.VMEM((slices + 1, 128, 128), F32)
    return pl.pallas_call(
        functools.partial(iterate_kernel, slices),
        out_shape=jax.ShapeDtypeStruct((UNITS, 1, STATE), F32),
        in_specs=[IN_VMEM] * (1 + len(operators)),
        out_specs=IN_VMEM,
        scratch_shapes=[pltpu.VMEM((32, 128), F32), pltpu.VMEM((FIELDS * 128, 128), F32)]
        + [coarse_shape] * 6,
        compiler_params=pltpu.CompilerParams(vmem_limit_bytes=VMEM_LIMIT),
        name="iterate",
    )(received, *operators)


def iterate_call(slices, received, volume_op, lift_op, coarse_volume, coarse_lift, mixing, restrict_op, prolong_op):
    operators = operators_call(
        volume_op, lift_op, coarse_volume, coarse_lift, mixing, restrict_op, prolong_op
    )
    return iterate_kernel_call(slices, received[:, None, :], operators)


def window_partners(slices, places):
    per_chip_row = 8
    depth = places // per_chip_row
    ring = 2 * depth
    route = []
    for slot in range(slices):
        for place in range(places):
            z = slot % 2 * depth + place // per_chip_row
            other = (z - 2 if z % 4 < 2 else z + 2) % ring
            partner = (slot - slot % 2 + other // depth) * places + other % depth * per_chip_row
            route.append((partner + place % per_chip_row, slot * places + place))
    return route


def on_device(
    initial,
    neighbours,
    volume_op,
    lift_op,
    coarse_volume,
    coarse_lift,
    mixing,
    restrict_op,
    prolong_op,
):
    params = pltpu.CompilerParams(vmem_limit_bytes=VMEM_LIMIT)
    route = window_partners(lax.axis_size("tm"), lax.axis_size("space"))
    state = initial.reshape(FIELDS * LAYER, -1)
    state_beside = lax.ppermute(state, ("tm", "space"), route)
    links_beside = lax.ppermute(neighbours, ("tm", "space"), route)
    block_shape = jax.ShapeDtypeStruct((UNITS, 1, 2 * STATE + 128), F32)
    half, basis = pl.pallas_call(
        own_modes_kernel,
        out_shape=(block_shape, jax.ShapeDtypeStruct((LAYER + 8, 128), F32)),
        in_specs=[IN_VMEM] * 2,
        out_specs=(pl.BlockSpec(memory_space=pl.ANY), IN_VMEM),
        scratch_shapes=[pltpu.VMEM((UNITS, 1, STATE), F32), pltpu.SemaphoreType.DMA],
        compiler_params=params,
        name="own_modes",
    )(state, neighbours)
    sent = pl.pallas_call(
        beside_modes_kernel,
        out_shape=block_shape,
        in_specs=[pl.BlockSpec(memory_space=pl.ANY)] + [IN_VMEM] * 3,
        out_specs=pl.BlockSpec(memory_space=pl.ANY),
        input_output_aliases={0: 0},
        scratch_shapes=[pltpu.VMEM((UNITS, 1, STATE + 128), F32), pltpu.SemaphoreType.DMA((FIELDS + 1,))],
        compiler_params=params,
        name="beside_modes",
    )(half, basis, state_beside, links_beside)
    windows = [[first + i for i in range(UNITS)] for first in range(0, lax.axis_size("space"), UNITS)]

    def exchange(blocks):
        return lax.all_to_all(blocks, "space", 0, 0, axis_index_groups=windows, tiled=True)

    received = exchange(sent)
    operators = operators_call(
        volume_op, lift_op, coarse_volume, coarse_lift, mixing, restrict_op, prolong_op
    )
    modes = iterate_kernel_call(lax.axis_size("tm"), received, operators)
    returned = exchange(modes)
    return pl.pallas_call(
        from_modes_kernel,
        out_shape=jax.ShapeDtypeStruct((1, FIELDS, LAYER, 128), F32),
        in_specs=[IN_VMEM] * 2,
        out_specs=pl.BlockSpec(memory_space=pl.ANY),
        scratch_shapes=[pltpu.VMEM((FIELDS, LAYER, 128), F32), pltpu.SemaphoreType.DMA((FIELDS,))],
        compiler_params=params,
        name="from_modes",
    )(returned, basis)


def solution(mesh):
    return jax.shard_map(
        on_device,
        mesh=mesh,
        in_specs=(P(None, None, "space"), P(None, "space"), P(), P(), P(), P(), P(), P(), P()),
        out_specs=P("tm", None, None, "space"),
        check_vma=False,
    )
```
